32 devices in a mesh: seq: 4 (over y, x), fsdp: 8 (over z, core).
Axes of the slice: x: 2, y: 2, z: 4, core: 2. Of those that a mesh axis runs over, the one named last changes fastest.
Arguments:
- inputs: bfloat16 [8, 512, 3072], P('fsdp', 'seq'), may hold values from -6 to 6
- w_qkv: bfloat16 [3072, 6144], P('fsdp', 'seq'), may hold values from -0.109375 to 0.109375
- saved_qkv: bfloat16 [8, 512, 6144], P('fsdp', 'seq'), may hold values from -60 to 60
- out_grad: bfloat16 [8, 512, 2048], P('fsdp', 'seq'), may hold values from -6 to 6
- clip_grid: int32 [8, 2, 3], P('fsdp'), may hold values from 1 to 2, as said below
- tile_pairs: int32 [8, 4, 6], P('fsdp'), may hold values from -1 to 3, as said below
Outputs:
- input_grad: bfloat16 [8, 512, 3072], P('fsdp', 'seq')
- weight_grad: float32 [3072, 6144], P('fsdp', 'seq')
The draws below stay inside these ranges and needn't reach their ends.
Inputs may be any that keep to these rules, and one draw needn't show every extreme that they name: `clip_grid`: in each group each clip has 1 x 2 or 2 x 1 tiles a frame (rows times columns is 2), the clips' tiles add up to 4, and group 0's clip 0 has one frame of 1 x 2 tiles. `tile_pairs`: the entries of query tile i, ascending and then -1, are exactly the tiles of i's clip whose frame, row and column tile indices differ from i's by at most one; they lie in tiles 2 * (i // 2 - 1) to 2 * (i // 2 + 2) - 1.
All inputs are finite; a program needn't handle non-finite values.
Results may differ from the reference program's by a relative error of at most 0.012.
The reference program's roundings to bfloat16 on the way count: a program that leaves them out, or rounds other values in their place, can miss the bound.
Values may be sent and summed in bfloat16 or wider, within the bound.
A program may use at most 128 MiB of HBM per device.

```python
import jax
import jax.numpy as jnp
from jax import lax

D = 3072
HD = 128
RT = 16
RH = 56
RW = 56
HEADS = 16
TT = 2
TH = 8
TW = 8
AREA = 2
CLIPS = 2
TILE = 128
KMAX = 6
QKV = 6144
SEQ_TOK = 512
NTILE = 4
GROUPS = 8
N_SEQ = 4


def tile_places_drawn(layout, tile_count):
    tile_sizes = layout[:, 0] * layout[:, 1] * layout[:, 2]
    clip_ends = jnp.cumsum(tile_sizes, dtype=jnp.int32).astype(jnp.int32)
    clip_starts = clip_ends - tile_sizes
    tile_ids = jnp.arange(tile_count, dtype=jnp.int32)
    member = ((tile_ids[:, None] >= clip_starts[None, :]) & (tile_ids[:, None] < clip_ends[None, :])).astype(jnp.int32)
    start_of = jnp.sum(member * clip_starts[None, :], axis=1, dtype=jnp.int32)
    rows_of = jnp.sum(member * layout[None, :, 1], axis=1, dtype=jnp.int32)
    cols_of = jnp.sum(member * layout[None, :, 2], axis=1, dtype=jnp.int32)
    clip_of = jnp.sum(member * jnp.arange(CLIPS, dtype=jnp.int32)[None, :], axis=1, dtype=jnp.int32)
    local_id = tile_ids - start_of
    within = local_id % (rows_of * cols_of)
    return (local_id // (rows_of * cols_of), within // cols_of, within % cols_of, clip_of)


def clip_layout(key):
    slab_count = NTILE // AREA
    first_frames = jax.random.randint(jax.random.fold_in(key, 11), (GROUPS,), 1, slab_count, dtype=jnp.int32)
    first_frames = first_frames.at[0].set(1)
    heights = jax.random.randint(jax.random.fold_in(key, 13), (GROUPS, CLIPS), 1, 3, dtype=jnp.int32)
    heights = heights.at[0].set(jnp.array([1, 2], dtype=jnp.int32))
    frames = jnp.stack([first_frames, slab_count - first_frames], axis=1)
    widths = AREA // heights
    return jnp.stack([frames, heights, widths], axis=2).astype(jnp.int32)


def group_pairs(layout):
    frame_tile, row_tile, column_tile, clip_tile = tile_places_drawn(layout, NTILE)
    tile_ids = jnp.arange(NTILE, dtype=jnp.int32)
    slot_ids = jnp.arange(KMAX, dtype=jnp.int32)
    place = ((tile_ids // AREA - 1) * AREA)[:, None] + slot_ids[None, :]
    inside = (place >= 0) & (place < NTILE)
    column = jnp.clip(place, 0, NTILE - 1)
    valid = inside & (clip_tile[column] == clip_tile[:, None])
    valid = valid & (jnp.abs(frame_tile[column] - frame_tile[:, None]) <= 1)
    valid = valid & (jnp.abs(row_tile[column] - row_tile[:, None]) <= 1)
    valid = valid & (jnp.abs(column_tile[column] - column_tile[:, None]) <= 1)
    order_key = jnp.where(valid, slot_ids[None, :], KMAX + slot_ids[None, :])
    order = jnp.argsort(order_key, axis=1, stable=True)
    listed = jnp.where(valid, place, -1)
    return jnp.take_along_axis(listed, order, axis=1).astype(jnp.int32)


def draw_clip_grid(key, part):
    return clip_layout(key)


def draw_tile_pairs(key, part):
    return jax.vmap(group_pairs)(clip_layout(key))


def draw_saved_qkv(key, part):
    key = jax.random.fold_in(key, 5)
    shape = (GROUPS, SEQ_TOK, 3 * HEADS * HD)
    base = jax.random.truncated_normal(jax.random.fold_in(key, 1), -6.0, 6.0, shape, jnp.float32)
    return base.astype(jnp.bfloat16)


def block_levels(stream_key, dims, split, smallest, largest):
    factor_of, own = 1.0, jax.random.fold_in(stream_key, 6)
    for axis_at, blocks in split:
        steps = jnp.exp(jax.random.uniform(jax.random.fold_in(own, axis_at), (blocks,), jnp.float32, smallest / len(split), largest / len(split)))
        factor_of = factor_of * jnp.repeat(steps, dims[axis_at] // blocks).reshape([-1 if axis == axis_at else 1 for axis in range(len(dims))])
    return factor_of


def centred(stream_key, dims, deviation, reach, cuts=(), kind=jnp.bfloat16):
    loudness = block_levels(stream_key, dims, cuts, -0.22, 0.18) if cuts else 1.0
    values = jax.random.normal(stream_key, dims, jnp.float32) * deviation * loudness
    return jnp.minimum(jnp.maximum(values, -reach), reach).astype(kind)


def setup_inputs(seed: int = 0) -> dict:
    seeds = jax.random.split(jax.random.key(seed), 7)
    inputs = centred(seeds[0], (GROUPS, SEQ_TOK, D), 1.0, 6.0, ((0, 8), (1, 4)))
    w_qkv = centred(seeds[1], (D, QKV), D ** -0.5, 0.109375, ((0, 8), (1, 4)))
    saved_qkv = draw_saved_qkv(jax.random.fold_in(seeds[6], 71), 0)
    out_grad = centred(seeds[3], (GROUPS, SEQ_TOK, HEADS * HD), 1.0, 6.0, ((0, 8), (1, 4)))
    clip_grid = draw_clip_grid(jax.random.fold_in(seeds[6], 71), 0)
    tile_pairs = draw_tile_pairs(jax.random.fold_in(seeds[6], 71), 0)
    return {"inputs": inputs, "w_qkv": w_qkv, "saved_qkv": saved_qkv, "out_grad": out_grad, "clip_grid": clip_grid, "tile_pairs": tile_pairs}


ROPE_BASE = 256.0

def tile_places(layout, tile_count):
    tile_sizes = layout[:, 0] * layout[:, 1] * layout[:, 2]
    clip_ends = jnp.cumsum(tile_sizes, dtype=jnp.int32).astype(jnp.int32)
    clip_starts = clip_ends - tile_sizes
    tile_ids = jnp.arange(tile_count, dtype=jnp.int32)
    member = ((tile_ids[:, None] >= clip_starts[None, :]) & (tile_ids[:, None] < clip_ends[None, :])).astype(jnp.int32)
    start_of = lax.optimization_barrier(jnp.sum(member * clip_starts[None, :], axis=1, dtype=jnp.int32))
    rows_of = lax.optimization_barrier(jnp.sum(member * layout[None, :, 1], axis=1, dtype=jnp.int32))
    cols_of = lax.optimization_barrier(jnp.sum(member * layout[None, :, 2], axis=1, dtype=jnp.int32))
    local_id = tile_ids - start_of
    within = local_id % (rows_of * cols_of)
    return (local_id // (rows_of * cols_of), within // cols_of, within % cols_of)

def rope_tables(layout, tile_count):
    frame_tile, row_tile, column_tile = tile_places(layout, tile_count)
    inside = jnp.arange(TILE, dtype=jnp.int32)
    frame_pos = (frame_tile[:, None] * TT + (inside // (TH * TW))[None, :]).reshape(-1)
    row_pos = (row_tile[:, None] * TH + (inside // TW % TH)[None, :]).reshape(-1)
    column_pos = (column_tile[:, None] * TW + (inside % TW)[None, :]).reshape(-1)
    angles = []
    for position, section in ((frame_pos, RT), (row_pos, RH), (column_pos, RW)):
        ladder = jnp.arange(section // 2, dtype=jnp.float32) * (2.0 / section)
        frequency = jnp.exp(-jnp.log(jnp.float32(ROPE_BASE)) * ladder)
        spin_angle = position.astype(jnp.float32)[:, None] * frequency[None, :]
        angles += [spin_angle, spin_angle]
    all_angles = jnp.concatenate(angles, axis=1)
    return (jnp.cos(all_angles), jnp.sin(all_angles))

def turn_half(values):
    pieces = []
    offset = 0
    for section in (RT, RH, RW):
        halfway = section // 2
        pieces += [-values[..., offset + halfway:offset + section], values[..., offset:offset + halfway]]
        offset += section
    return jnp.concatenate(pieces, axis=-1)

def rotate(values, cosine_table, sine_table):
    return values * cosine_table + turn_half(values) * sine_table

def unrotate(values, cosine_table, sine_table):
    return values * cosine_table - turn_half(values * sine_table)

def head_backward(query_rows, key_rows, value_rows, grad_rows, window, cosine_table, sine_table):
    tile_count, slot_count = window.shape
    scale = HD ** (-0.5)
    rot_q = rotate(query_rows.astype(jnp.float32), cosine_table, sine_table).astype(jnp.bfloat16)
    rot_k = rotate(key_rows.astype(jnp.float32), cosine_table, sine_table).astype(jnp.bfloat16)
    live_slot = window >= 0
    safe_slot = jnp.where(live_slot, window, 0).astype(jnp.int32)
    tile_q = rot_q.reshape(tile_count, TILE, HD).astype(jnp.float32)
    tile_k = rot_k.reshape(tile_count, TILE, HD)[safe_slot].reshape(tile_count, slot_count * TILE, HD).astype(jnp.float32)
    tile_v = value_rows.reshape(tile_count, TILE, HD)[safe_slot].reshape(tile_count, slot_count * TILE, HD).astype(jnp.float32)
    tile_g = grad_rows.reshape(tile_count, TILE, HD).astype(jnp.float32)
    keep_mask = jnp.repeat(live_slot, TILE, axis=1)[:, None, :]
    scores = jnp.einsum('ntd,nkd->ntk', tile_q, tile_k) * scale
    scores = jnp.where(keep_mask, scores, -jnp.inf)
    highest = lax.optimization_barrier(jnp.max(scores, axis=-1, keepdims=True))
    expo_terms = jnp.exp(scores - highest)
    probs_full = expo_terms / lax.optimization_barrier(jnp.sum(expo_terms, axis=-1, keepdims=True))
    probs_low = lax.optimization_barrier(probs_full.astype(jnp.bfloat16)).astype(jnp.float32)
    value_part = jnp.einsum('ntk,ntd->nkd', probs_low, tile_g).reshape(tile_count, slot_count, TILE, HD)
    value_grad = jnp.zeros((tile_count, TILE, HD), jnp.float32).at[safe_slot].add(value_part)
    prob_grad = jnp.einsum('ntd,nkd->ntk', tile_g, tile_v)
    row_total = lax.optimization_barrier(jnp.sum(probs_full * prob_grad, axis=-1, keepdims=True))
    score_grad = lax.optimization_barrier((probs_full * (prob_grad - row_total) * scale).astype(jnp.bfloat16)).astype(jnp.float32)
    query_grad = jnp.einsum('ntk,nkd->ntd', score_grad, tile_k).reshape(-1, HD)
    key_part = jnp.einsum('ntk,ntd->nkd', score_grad, tile_q).reshape(tile_count, slot_count, TILE, HD)
    key_grad = jnp.zeros((tile_count, TILE, HD), jnp.float32).at[safe_slot].add(key_part).reshape(-1, HD)
    return (unrotate(query_grad, cosine_table, sine_table).astype(jnp.bfloat16), unrotate(key_grad, cosine_table, sine_table).astype(jnp.bfloat16), value_grad.reshape(-1, HD).astype(jnp.bfloat16))

def reference(inputs, w_qkv, saved_qkv, out_grad, clip_grid, tile_pairs):
    block_cols = HEADS // N_SEQ * 3 * HD

    def group_backward(item):
        qkv_rows, grad_rows, layout, window = item
        cosine_table, sine_table = rope_tables(layout, NTILE)
        per_head = qkv_rows.reshape(SEQ_TOK, HEADS, 3, HD).transpose(1, 2, 0, 3)
        head_grads = grad_rows.reshape(SEQ_TOK, HEADS, HD).transpose(1, 0, 2)

        def one_head(head_item):
            trio_rows, grad_head = head_item
            return head_backward(trio_rows[0], trio_rows[1], trio_rows[2], grad_head, window, cosine_table, sine_table)
        d_query, d_key, d_value = lax.map(one_head, (per_head, head_grads))
        stacked = jnp.stack([d_query, d_key, d_value], axis=1)
        return stacked.transpose(2, 0, 1, 3).reshape(SEQ_TOK, HEADS * 3 * HD)
    qkv_grad = lax.map(group_backward, (saved_qkv, out_grad, clip_grid, tile_pairs))

    def add_group(running, item):
        group_inputs, group_grads = item
        partial_sum = lax.dot_general(group_inputs, group_grads, (((0,), (0,)), ((), ())), preferred_element_type=jnp.float32)
        return (running + lax.optimization_barrier(partial_sum.astype(jnp.bfloat16)).astype(jnp.float32), None)
    weight_grad = lax.scan(add_group, jnp.zeros((D, HEADS * 3 * HD), jnp.float32), (inputs, qkv_grad))[0]
    weight_blocks = w_qkv.reshape(D, N_SEQ, block_cols).transpose(1, 0, 2)

    def group_input_grad(group_grads):
        grad_blocks = group_grads.reshape(SEQ_TOK, N_SEQ, block_cols).transpose(1, 0, 2)

        def add_block(running, item):
            grad_block, weight_block = item
            partial_sum = lax.dot_general(grad_block, weight_block, (((1,), (1,)), ((), ())), preferred_element_type=jnp.float32)
            return (running + lax.optimization_barrier(partial_sum.astype(jnp.bfloat16)).astype(jnp.float32), None)
        summed = lax.scan(add_block, jnp.zeros((SEQ_TOK, D), jnp.float32), (grad_blocks, weight_blocks))[0]
        return summed.astype(jnp.bfloat16)
    input_grad = lax.map(group_input_grad, qkv_grad)
    return (input_grad, weight_grad)
```

```python
import functools

import jax
import jax.numpy as jnp
from jax import lax
from jax.experimental import pallas as pl
from jax.experimental.pallas import tpu as pltpu
from jax.sharding import PartitionSpec as P

HD = 128
RT = 16
RH = 56
RW = 56
TT = 2
TH = 8
TW = 8
AREA = 2
TILE = 128


ROPE_BASE = 256.0


def tile_places(layout, tile_count):
    tile_sizes = layout[:, 0] * layout[:, 1] * layout[:, 2]
    clip_ends = jnp.cumsum(tile_sizes, dtype=jnp.int32)
    clip_starts = clip_ends - tile_sizes
    tile_ids = jnp.arange(tile_count, dtype=jnp.int32)
    member = (
        (tile_ids[:, None] >= clip_starts[None, :]) & (tile_ids[:, None] < clip_ends[None, :])
    ).astype(jnp.int32)
    start_of = jnp.sum(member * clip_starts[None, :], axis=1, dtype=jnp.int32)
    rows_of = jnp.sum(member * layout[None, :, 1], axis=1, dtype=jnp.int32)
    cols_of = jnp.sum(member * layout[None, :, 2], axis=1, dtype=jnp.int32)
    local_id = tile_ids - start_of
    within = local_id % (rows_of * cols_of)
    return (local_id // (rows_of * cols_of), within // cols_of, within % cols_of)


def rope_tables(layout, tile_count):
    frame_tile, row_tile, column_tile = tile_places(layout, tile_count)
    inside = jnp.arange(TILE, dtype=jnp.int32)
    frame_pos = (frame_tile[:, None] * TT + (inside // (TH * TW))[None, :]).reshape(-1)
    row_pos = (row_tile[:, None] * TH + (inside // TW % TH)[None, :]).reshape(-1)
    column_pos = (column_tile[:, None] * TW + (inside % TW)[None, :]).reshape(-1)
    angles = []
    for position, section in ((frame_pos, RT), (row_pos, RH), (column_pos, RW)):
        ladder = jnp.arange(section // 2, dtype=jnp.float32) * (2.0 / section)
        frequency = jnp.exp(-jnp.log(jnp.float32(ROPE_BASE)) * ladder)
        spin_angle = position.astype(jnp.float32)[:, None] * frequency[None, :]
        angles += [spin_angle, spin_angle]
    all_angles = jnp.concatenate(angles, axis=1)
    signs = []
    for section in (RT, RH, RW):
        signs += [-jnp.ones((section // 2,), jnp.float32), jnp.ones((section // 2,), jnp.float32)]
    return (jnp.cos(all_angles), jnp.sin(all_angles) * jnp.concatenate(signs)[None, :])


def partner(values):
    lane = lax.broadcasted_iota(jnp.int32, values.shape, 1)
    short, long = RT // 2, RH // 2
    first = (lane < RT + long) | ((lane >= RT + RH) & (lane < RT + RH + long))
    wide = jnp.where(
        first, pltpu.roll(values, HD - long, 1), pltpu.roll(values, long, 1)
    )
    narrow = jnp.where(
        lane < short, pltpu.roll(values, HD - short, 1), pltpu.roll(values, short, 1)
    )
    return jnp.where(lane < RT, narrow, wide)


def attention_kernel(qkv_ref, grad_ref, cos_ref, sin_ref, bias_ref, out_ref, dk_ref, dv_ref):
    rows = AREA * TILE
    slabs = qkv_ref.shape[0] // rows
    scale = HD ** (-0.5)
    cosine, sine = cos_ref[...], sin_ref[...]

    def rotated(start):
        values = qkv_ref[:, start : start + HD].astype(jnp.float32)
        return (values * cosine + partner(values) * sine).astype(jnp.bfloat16)

    rot_q, rot_k = rotated(0), rotated(HD)
    values = qkv_ref[:, 2 * HD : 3 * HD]
    grads = grad_ref[...]
    across = (((1,), (1,)), ((), ()))
    plain = (((1,), (0,)), ((), ()))
    down = (((0,), (0,)), ((), ()))
    dk_ref[...] = jnp.zeros_like(dk_ref)
    dv_ref[...] = jnp.zeros_like(dv_ref)
    for slab in range(slabs):
        here = slice(slab * rows, (slab + 1) * rows)
        near = slice(max(0, slab - 1) * rows, min(slabs, slab + 2) * rows)
        width = near.stop - near.start
        query, grad, key, value = rot_q[here], grads[here], rot_k[near], values[near]
        bias = jnp.concatenate(
            [
                jnp.broadcast_to(bias_ref[tile : tile + 1, near], (TILE, width))
                for tile in range(slab * AREA, (slab + 1) * AREA)
            ],
            axis=0,
        )
        scores = lax.dot_general(query, key, across, preferred_element_type=jnp.float32)
        scores = scores * scale + bias
        expo = jnp.exp(scores - jnp.max(scores, axis=-1, keepdims=True))
        probs = expo * (1.0 / jnp.sum(expo, axis=-1, keepdims=True))
        dv_ref[near, :] += lax.dot_general(
            probs.astype(jnp.bfloat16), grad, down, preferred_element_type=jnp.float32
        )
        prob_grad = lax.dot_general(grad, value, across, preferred_element_type=jnp.float32)
        total = jnp.sum(probs * prob_grad, axis=-1, keepdims=True)
        score_grad = (probs * (prob_grad - total) * scale).astype(jnp.bfloat16)
        dq = lax.dot_general(score_grad, key, plain, preferred_element_type=jnp.float32)
        dq = dq * cosine[here] - partner(dq) * sine[here]
        out_ref[here, 0:HD] = dq.astype(jnp.bfloat16)
        dk_ref[near, :] += lax.dot_general(
            score_grad, query, down, preferred_element_type=jnp.float32
        )
    dk = dk_ref[...]
    out_ref[:, HD : 2 * HD] = (dk * cosine - partner(dk) * sine).astype(jnp.bfloat16)
    out_ref[:, 2 * HD : 3 * HD] = dv_ref[...].astype(jnp.bfloat16)


def attention(mixed, cosine, sine, bias):
    tokens = mixed.shape[0]
    heads = mixed.shape[1] // (4 * HD)
    whole = lambda array: pl.BlockSpec(array.shape, lambda head: (0, 0))
    return pl.pallas_call(
        attention_kernel,
        grid=(heads,),
        out_shape=jax.ShapeDtypeStruct((tokens, heads * 3 * HD), jnp.bfloat16),
        in_specs=[
            pl.BlockSpec((tokens, 3 * HD), lambda head: (0, head)),
            pl.BlockSpec((tokens, HD), lambda head: (0, 3 * heads + head)),
            whole(cosine),
            whole(sine),
            whole(bias),
        ],
        out_specs=pl.BlockSpec((tokens, 3 * HD), lambda head: (0, head)),
        scratch_shapes=[
            pltpu.VMEM((tokens, HD), jnp.float32),
            pltpu.VMEM((tokens, HD), jnp.float32),
        ],
        compiler_params=pltpu.CompilerParams(vmem_limit_bytes=48 * 1024 * 1024),
        cost_estimate=pl.CostEstimate(
            flops=heads * 10 * tokens * min(tokens, 768) * HD,
            bytes_accessed=16 * heads * tokens * HD,
            transcendentals=heads * tokens * min(tokens, 768),
        ),
    )(mixed, mixed, cosine, sine, bias)


def by_device(rows, parts):
    tokens, columns = rows.shape
    return rows.reshape(tokens, parts, columns // parts).transpose(1, 0, 2)


def body(seq_size, fsdp_size, inputs, w_qkv, saved_qkv, out_grad, clip_grid, tile_pairs):
    window = tile_pairs[0]
    tile_count = window.shape[0]
    mixed = jnp.concatenate(
        [by_device(saved_qkv[0], seq_size), by_device(out_grad[0], seq_size)], axis=2
    )
    mixed = lax.all_to_all(mixed, "seq", split_axis=0, concat_axis=0, tiled=True)
    mixed = mixed.reshape(-1, mixed.shape[2])
    weight_full = lax.all_gather(w_qkv, "fsdp", axis=0, tiled=True)
    group_rows = lax.all_gather(inputs[0], "seq", axis=0, tiled=True)
    cosine, sine = rope_tables(clip_grid[0], tile_count)
    listed = jnp.any(
        window[:, :, None] == jnp.arange(tile_count, dtype=jnp.int32)[None, None, :], axis=1
    )
    bias = jnp.repeat(jnp.where(listed, 0.0, -1e30).astype(jnp.float32), TILE, axis=1)
    qkv_grad = attention(mixed, cosine, sine, bias)
    weight_part = lax.psum_scatter(
        lax.dot_general(
            group_rows, qkv_grad, (((0,), (0,)), ((), ())), preferred_element_type=jnp.float32
        ).astype(jnp.bfloat16),
        "fsdp",
        scatter_dimension=0,
        tiled=True,
    ).astype(jnp.float32)
    input_part = lax.psum_scatter(
        lax.dot_general(
            qkv_grad, weight_full, (((1,), (1,)), ((), ())), preferred_element_type=jnp.float32
        ).astype(jnp.bfloat16),
        "seq",
        scatter_dimension=0,
        tiled=True,
    )
    return (input_part[None], weight_part)


def solution(mesh):
    in_specs = (
        P("fsdp", "seq", None),
        P("fsdp", "seq"),
        P("fsdp", "seq", None),
        P("fsdp", "seq", None),
        P("fsdp", None, None),
        P("fsdp", None, None),
    )
    out_specs = (P("fsdp", "seq", None), P("fsdp", "seq"))
    local = functools.partial(body, mesh.shape["seq"], mesh.shape["fsdp"])
    return jax.shard_map(local, mesh=mesh, in_specs=in_specs, out_specs=out_specs, check_vma=False)
```

```python
import functools

import jax
import jax.numpy as jnp
from jax import lax
from jax.experimental import pallas as pl
from jax.experimental.pallas import tpu as pltpu
from jax.sharding import PartitionSpec as P

HD = 128
RT = 16
RH = 56
RW = 56
TT = 2
TH = 8
TW = 8
AREA = 2
TILE = 128


ROPE_BASE = 256.0


def tile_places(layout, tile_count):
    tile_sizes = layout[:, 0] * layout[:, 1] * layout[:, 2]
    clip_ends = jnp.cumsum(tile_sizes, dtype=jnp.int32)
    clip_starts = clip_ends - tile_sizes
    tile_ids = jnp.arange(tile_count, dtype=jnp.int32)
    member = (
        (tile_ids[:, None] >= clip_starts[None, :]) & (tile_ids[:, None] < clip_ends[None, :])
    ).astype(jnp.int32)
    start_of = jnp.sum(member * clip_starts[None, :], axis=1, dtype=jnp.int32)
    rows_of = jnp.sum(member * layout[None, :, 1], axis=1, dtype=jnp.int32)
    cols_of = jnp.sum(member * layout[None, :, 2], axis=1, dtype=jnp.int32)
    local_id = tile_ids - start_of
    within = local_id % (rows_of * cols_of)
    return (local_id // (rows_of * cols_of), within // cols_of, within % cols_of)


def rope_tables(layout, tile_count):
    frame_tile, row_tile, column_tile = tile_places(layout, tile_count)
    inside = jnp.arange(TILE, dtype=jnp.int32)
    frame_pos = (frame_tile[:, None] * TT + (inside // (TH * TW))[None, :]).reshape(-1)
    row_pos = (row_tile[:, None] * TH + (inside // TW % TH)[None, :]).reshape(-1)
    column_pos = (column_tile[:, None] * TW + (inside % TW)[None, :]).reshape(-1)
    angles = []
    for position, section in ((frame_pos, RT), (row_pos, RH), (column_pos, RW)):
        ladder = jnp.arange(section // 2, dtype=jnp.float32) * (2.0 / section)
        frequency = jnp.exp(-jnp.log(jnp.float32(ROPE_BASE)) * ladder)
        spin_angle = position.astype(jnp.float32)[:, None] * frequency[None, :]
        angles += [spin_angle, spin_angle]
    all_angles = jnp.concatenate(angles, axis=1)
    signs = []
    for section in (RT, RH, RW):
        signs += [-jnp.ones((section // 2,), jnp.float32), jnp.ones((section // 2,), jnp.float32)]
    return (jnp.cos(all_angles), jnp.sin(all_angles) * jnp.concatenate(signs)[None, :])


def partner(values):
    lane = lax.broadcasted_iota(jnp.int32, values.shape, 1)
    short, long = RT // 2, RH // 2
    first = (lane < RT + long) | ((lane >= RT + RH) & (lane < RT + RH + long))
    wide = jnp.where(
        first, pltpu.roll(values, HD - long, 1), pltpu.roll(values, long, 1)
    )
    narrow = jnp.where(
        lane < short, pltpu.roll(values, HD - short, 1), pltpu.roll(values, short, 1)
    )
    return jnp.where(lane < RT, narrow, wide)


def head_backward(qkv_ref, grad_ref, cos_ref, sin_ref, bias_ref, out_ref, dk_ref, dv_ref, head):
    rows = AREA * TILE
    slabs = qkv_ref.shape[0] // rows
    scale = HD ** (-0.5)
    cosine, sine = cos_ref[...], sin_ref[...]

    def lanes(start, count=HD):
        return pl.ds(pl.multiple_of(start, HD), count)

    def rotated(start):
        values = qkv_ref[:, lanes(start)].astype(jnp.float32)
        return (values * cosine + partner(values) * sine).astype(jnp.bfloat16)

    base = head * (3 * HD)
    rot_q, rot_k = rotated(base), rotated(base + HD)
    values = qkv_ref[:, lanes(base + 2 * HD)]
    grads = grad_ref[:, lanes(head * HD)]
    across = (((1,), (1,)), ((), ()))
    plain = (((1,), (0,)), ((), ()))
    down = (((0,), (0,)), ((), ()))
    dk_ref[...] = jnp.zeros_like(dk_ref)
    dv_ref[...] = jnp.zeros_like(dv_ref)
    for slab in range(slabs):
        here = slice(slab * rows, (slab + 1) * rows)
        near = slice(max(0, slab - 1) * rows, min(slabs, slab + 2) * rows)
        width = near.stop - near.start
        query, grad, key, value = rot_q[here], grads[here], rot_k[near], values[near]
        bias = jnp.concatenate(
            [
                jnp.broadcast_to(bias_ref[tile : tile + 1, near], (TILE, width))
                for tile in range(slab * AREA, (slab + 1) * AREA)
            ],
            axis=0,
        )
        scores = lax.dot_general(query, key, across, preferred_element_type=jnp.float32)
        scores = scores * scale + bias
        expo = jnp.exp(scores - jnp.max(scores, axis=-1, keepdims=True))
        probs = expo * (1.0 / jnp.sum(expo, axis=-1, keepdims=True))
        dv_ref[near, :] += lax.dot_general(
            probs.astype(jnp.bfloat16), grad, down, preferred_element_type=jnp.float32
        )
        prob_grad = lax.dot_general(grad, value, across, preferred_element_type=jnp.float32)
        total = jnp.sum(probs * prob_grad, axis=-1, keepdims=True)
        score_grad = (probs * (prob_grad - total) * scale).astype(jnp.bfloat16)
        dq = lax.dot_general(score_grad, key, plain, preferred_element_type=jnp.float32)
        dq = dq * cosine[here] - partner(dq) * sine[here]
        out_ref[here, lanes(base)] = dq.astype(jnp.bfloat16)
        dk_ref[near, :] += lax.dot_general(
            score_grad, query, down, preferred_element_type=jnp.float32
        )
    dk = dk_ref[...]
    out_ref[:, lanes(base + HD)] = (dk * cosine - partner(dk) * sine).astype(jnp.bfloat16)
    out_ref[:, lanes(base + 2 * HD)] = dv_ref[...].astype(jnp.bfloat16)


def greet(axis, others):
    barrier = pltpu.get_barrier_semaphore()
    for other in others:
        pl.semaphore_signal(
            barrier, inc=1, device_id={axis: other}, device_id_type=pl.DeviceIdType.MESH
        )
    pl.semaphore_wait(barrier, len(others))


def attention_kernel(
    size, inputs_ref, saved_ref, gout_ref, cos_ref, sin_ref, bias_ref, out_ref, rows_ref,
    qkv_ref, grad_ref, dk_ref, dv_ref, send_sems, recv_sems, own_sems, send_rows, recv_rows,
):
    me = lax.axis_index("seq")
    tokens, columns = saved_ref.shape
    heads = columns // size // (3 * HD)
    others = [lax.rem(me + step, size) for step in range(1, size)]
    greet("seq", others)
    mine = pl.ds(pl.multiple_of(me * tokens, TILE), tokens)
    parts = ((saved_ref, qkv_ref, 3 * HD), (gout_ref, grad_ref, HD))

    def remote(source, target, send, recv, other):
        return pltpu.make_async_remote_copy(
            src_ref=source, dst_ref=target, send_sem=send, recv_sem=recv,
            device_id={"seq": other}, device_id_type=pl.DeviceIdType.MESH,
        )

    def piece(head, step, at):
        source, target, width = parts[at]
        other = others[step]
        there = pl.ds(pl.multiple_of((other * heads + head) * width, HD), width)
        here = pl.ds(pl.multiple_of(head * width, HD), width)
        return remote(
            source.at[:, there], target.at[mine, here],
            send_sems.at[head, step, at], recv_sems.at[head, step, at], other,
        )

    def own(head, at):
        source, target, width = parts[at]
        there = pl.ds(pl.multiple_of((me * heads + head) * width, HD), width)
        here = pl.ds(pl.multiple_of(head * width, HD), width)
        return pltpu.make_async_copy(
            source.at[:, there], target.at[mine, here], own_sems.at[head, at]
        )

    own_rows = pltpu.make_async_copy(inputs_ref, rows_ref.at[mine], own_sems.at[heads, 0])
    all_rows = [
        remote(inputs_ref, rows_ref.at[mine], send_rows.at[step], recv_rows.at[step], others[step])
        for step in range(size - 1)
    ]

    def launch(head, carry):
        for at in range(2):
            own(head, at).start()
        for step in range(size - 1):
            for at in range(2):
                piece(head, step, at).start()
        return carry

    lax.fori_loop(0, heads, launch, 0)
    for copy in all_rows:
        copy.start()
    own_rows.start()

    def work(head, carry):
        for at in range(2):
            own(head, at).wait()
        for step in range(size - 1):
            for at in range(2):
                piece(head, step, at).wait()
        head_backward(
            qkv_ref, grad_ref, cos_ref, sin_ref, bias_ref, out_ref, dk_ref, dv_ref, head
        )
        return carry

    lax.fori_loop(0, heads, work, 0)
    own_rows.wait()
    for copy in all_rows:
        copy.wait()


def attention(size, inputs, saved, gout, cosine, sine, bias):
    tokens = inputs.shape[0] * size
    heads = gout.shape[1] // size // HD
    vmem, anywhere = pl.BlockSpec(memory_space=pltpu.VMEM), pl.BlockSpec(memory_space=pl.ANY)
    dma = pltpu.SemaphoreType.DMA
    return pl.pallas_call(
        functools.partial(attention_kernel, size),
        out_shape=(
            jax.ShapeDtypeStruct((tokens, heads * 3 * HD), jnp.bfloat16),
            jax.ShapeDtypeStruct((tokens, inputs.shape[1]), jnp.bfloat16),
        ),
        in_specs=[anywhere] * 3 + [vmem] * 3,
        out_specs=(vmem, anywhere),
        scratch_shapes=[
            pltpu.VMEM((tokens, heads * 3 * HD), jnp.bfloat16),
            pltpu.VMEM((tokens, heads * HD), jnp.bfloat16),
            pltpu.VMEM((tokens, HD), jnp.float32),
            pltpu.VMEM((tokens, HD), jnp.float32),
            dma((heads, size - 1, 2)),
            dma((heads, size - 1, 2)),
            dma((heads + 1, 2)),
            dma((size - 1,)),
            dma((size - 1,)),
        ],
        compiler_params=pltpu.CompilerParams(
            collective_id=0, has_side_effects=True, vmem_limit_bytes=48 * 1024 * 1024
        ),
        cost_estimate=pl.CostEstimate(
            flops=heads * 10 * tokens * min(tokens, 768) * HD,
            bytes_accessed=100 * 1024 * 1024,
            transcendentals=heads * tokens * min(tokens, 768),
        ),
    )(inputs, saved, gout, cosine, sine, bias)


def input_kernel(size, grad_ref, weight_ref, out_ref, sent, landed, send_sems, recv_sems):
    me = lax.axis_index("seq")
    chunks, width = sent.shape[0], sent.shape[2]
    tokens = out_ref.shape[0]
    others = [lax.rem(me + step, size) for step in range(1, size)]
    greet("seq", others)

    def piece(chunk, step):
        there = pl.ds(pl.multiple_of(others[step] * tokens, TILE), tokens)
        return pltpu.make_async_remote_copy(
            src_ref=sent.at[chunk, there], dst_ref=landed.at[chunk, step],
            send_sem=send_sems.at[chunk, step], recv_sem=recv_sems.at[chunk, step],
            device_id={"seq": others[step]}, device_id_type=pl.DeviceIdType.MESH,
        )

    def product(chunk, carry):
        here = pl.ds(pl.multiple_of(chunk * width, HD), width)
        sent[chunk] = lax.dot_general(
            grad_ref[...], weight_ref[here, :], (((1,), (1,)), ((), ())),
            preferred_element_type=jnp.float32,
        ).astype(jnp.bfloat16)
        for step in range(size - 1):
            piece(chunk, step).start()
        return carry

    def add(chunk, carry):
        here = pl.ds(pl.multiple_of(chunk * width, HD), width)
        mine = pl.ds(pl.multiple_of(me * tokens, TILE), tokens)
        total = sent[chunk, mine].astype(jnp.float32)
        for step in range(size - 1):
            piece(chunk, step).wait()
            total = total + landed[chunk, step].astype(jnp.float32)
        out_ref[:, here] = total.astype(jnp.bfloat16)
        return carry

    lax.fori_loop(0, chunks, product, 0)
    lax.fori_loop(0, chunks, add, 0)


def input_part(size, qkv_grad, weight):
    tokens, depth = qkv_grad.shape
    model = weight.shape[0]
    width = 3 * HD
    chunks = model // width
    vmem = pl.BlockSpec(memory_space=pltpu.VMEM)
    dma = pltpu.SemaphoreType.DMA
    return pl.pallas_call(
        functools.partial(input_kernel, size),
        out_shape=jax.ShapeDtypeStruct((tokens // size, model), jnp.bfloat16),
        in_specs=[vmem, vmem],
        out_specs=vmem,
        scratch_shapes=[
            pltpu.VMEM((chunks, tokens, width), jnp.bfloat16),
            pltpu.VMEM((chunks, size - 1, tokens // size, width), jnp.bfloat16),
            dma((chunks, size - 1)),
            dma((chunks, size - 1)),
        ],
        compiler_params=pltpu.CompilerParams(
            collective_id=1, has_side_effects=True, vmem_limit_bytes=56 * 1024 * 1024
        ),
        cost_estimate=pl.CostEstimate(
            flops=2 * tokens * depth * model, bytes_accessed=100 * 1024 * 1024, transcendentals=0
        ),
    )(qkv_grad, weight)


def body(seq_size, inputs, w_qkv, saved_qkv, out_grad, clip_grid, tile_pairs):
    window = tile_pairs[0]
    tile_count = window.shape[0]
    weight_full = lax.all_gather(w_qkv, "fsdp", axis=0, tiled=True)
    cosine, sine = rope_tables(clip_grid[0], tile_count)
    listed = jnp.any(
        window[:, :, None] == jnp.arange(tile_count, dtype=jnp.int32)[None, None, :], axis=1
    )
    bias = jnp.repeat(jnp.where(listed, 0.0, -1e30).astype(jnp.float32), TILE, axis=1)
    qkv_grad, group_rows = attention(
        seq_size, inputs[0], saved_qkv[0], out_grad[0], cosine, sine, bias
    )
    product = lax.dot_general(
        group_rows, qkv_grad, (((0,), (0,)), ((), ())), preferred_element_type=jnp.float32
    ).astype(jnp.bfloat16)
    weight_part = lax.psum_scatter(product, "fsdp", scatter_dimension=0, tiled=True)
    input_grad = input_part(seq_size, qkv_grad, weight_full)
    return (input_grad[None], weight_part.astype(jnp.float32))


def solution(mesh):
    in_specs = (
        P("fsdp", "seq", None),
        P("fsdp", "seq"),
        P("fsdp", "seq", None),
        P("fsdp", "seq", None),
        P("fsdp", None, None),
        P("fsdp", None, None),
    )
    out_specs = (P("fsdp", "seq", None), P("fsdp", "seq"))
    local = functools.partial(body, mesh.shape["seq"])
    return jax.shard_map(local, mesh=mesh, in_specs=in_specs, out_specs=out_specs, check_vma=False)
```

```python
import functools

import jax
import jax.numpy as jnp
from jax import lax
from jax.experimental import pallas as pl
from jax.experimental.pallas import tpu as pltpu
from jax.sharding import PartitionSpec as P

HD = 128
RT = 16
RH = 56
RW = 56
TT = 2
TH = 8
TW = 8
AREA = 2
TILE = 128


ROPE_BASE = 256.0


def tile_places(layout, tile_count):
    tile_sizes = layout[:, 0] * layout[:, 1] * layout[:, 2]
    clip_ends = jnp.cumsum(tile_sizes, dtype=jnp.int32)
    clip_starts = clip_ends - tile_sizes
    tile_ids = jnp.arange(tile_count, dtype=jnp.int32)
    member = (
        (tile_ids[:, None] >= clip_starts[None, :]) & (tile_ids[:, None] < clip_ends[None, :])
    ).astype(jnp.int32)
    start_of = jnp.sum(member * clip_starts[None, :], axis=1, dtype=jnp.int32)
    rows_of = jnp.sum(member * layout[None, :, 1], axis=1, dtype=jnp.int32)
    cols_of = jnp.sum(member * layout[None, :, 2], axis=1, dtype=jnp.int32)
    local_id = tile_ids - start_of
    within = local_id % (rows_of * cols_of)
    return (local_id // (rows_of * cols_of), within // cols_of, within % cols_of)


def rope_tables(layout, tile_count):
    frame_tile, row_tile, column_tile = tile_places(layout, tile_count)
    inside = jnp.arange(TILE, dtype=jnp.int32)
    frame_pos = (frame_tile[:, None] * TT + (inside // (TH * TW))[None, :]).reshape(-1)
    row_pos = (row_tile[:, None] * TH + (inside // TW % TH)[None, :]).reshape(-1)
    column_pos = (column_tile[:, None] * TW + (inside % TW)[None, :]).reshape(-1)
    angles = []
    for position, section in ((frame_pos, RT), (row_pos, RH), (column_pos, RW)):
        ladder = jnp.arange(section // 2, dtype=jnp.float32) * (2.0 / section)
        frequency = jnp.exp(-jnp.log(jnp.float32(ROPE_BASE)) * ladder)
        spin_angle = position.astype(jnp.float32)[:, None] * frequency[None, :]
        angles += [spin_angle, spin_angle]
    all_angles = jnp.concatenate(angles, axis=1)
    signs = []
    for section in (RT, RH, RW):
        signs += [-jnp.ones((section // 2,), jnp.float32), jnp.ones((section // 2,), jnp.float32)]
    return (jnp.cos(all_angles), jnp.sin(all_angles) * jnp.concatenate(signs)[None, :])


def partner(values):
    lane = lax.broadcasted_iota(jnp.int32, values.shape, 1)
    short, long = RT // 2, RH // 2
    first = (lane < RT + long) | ((lane >= RT + RH) & (lane < RT + RH + long))
    wide = jnp.where(
        first, pltpu.roll(values, HD - long, 1), pltpu.roll(values, long, 1)
    )
    narrow = jnp.where(
        lane < short, pltpu.roll(values, HD - short, 1), pltpu.roll(values, short, 1)
    )
    return jnp.where(lane < RT, narrow, wide)


def head_backward(qkv_ref, grad_ref, cos_ref, sin_ref, bias_ref, out_ref, dk_ref, dv_ref, head):
    rows = AREA * TILE
    slabs = qkv_ref.shape[0] // rows
    scale = HD ** (-0.5)
    cosine, sine = cos_ref[...], sin_ref[...]

    def lanes(start, count=HD):
        return pl.ds(pl.multiple_of(start, HD), count)

    def rotated(start):
        values = qkv_ref[:, lanes(start)].astype(jnp.float32)
        return (values * cosine + partner(values) * sine).astype(jnp.bfloat16)

    base = head * (3 * HD)
    rot_q, rot_k = rotated(base), rotated(base + HD)
    values = qkv_ref[:, lanes(base + 2 * HD)]
    grads = grad_ref[:, lanes(head * HD)]
    across = (((1,), (1,)), ((), ()))
    plain = (((1,), (0,)), ((), ()))
    down = (((0,), (0,)), ((), ()))
    dk_ref[...] = jnp.zeros_like(dk_ref)
    dv_ref[...] = jnp.zeros_like(dv_ref)
    for slab in range(slabs):
        here = slice(slab * rows, (slab + 1) * rows)
        near = slice(max(0, slab - 1) * rows, min(slabs, slab + 2) * rows)
        width = near.stop - near.start
        query, grad, key, value = rot_q[here], grads[here], rot_k[near], values[near]
        bias = jnp.concatenate(
            [
                jnp.broadcast_to(bias_ref[tile : tile + 1, near], (TILE, width))
                for tile in range(slab * AREA, (slab + 1) * AREA)
            ],
            axis=0,
        )
        scores = lax.dot_general(query, key, across, preferred_element_type=jnp.float32)
        scores = scores * scale + bias
        expo = jnp.exp(scores - jnp.max(scores, axis=-1, keepdims=True))
        probs = expo * (1.0 / jnp.sum(expo, axis=-1, keepdims=True))
        dv_ref[near, :] += lax.dot_general(
            probs.astype(jnp.bfloat16), grad, down, preferred_element_type=jnp.float32
        )
        prob_grad = lax.dot_general(grad, value, across, preferred_element_type=jnp.float32)
        total = jnp.sum(probs * prob_grad, axis=-1, keepdims=True)
        score_grad = (probs * (prob_grad - total) * scale).astype(jnp.bfloat16)
        dq = lax.dot_general(score_grad, key, plain, preferred_element_type=jnp.float32)
        dq = dq * cosine[here] - partner(dq) * sine[here]
        out_ref[here, lanes(base)] = dq.astype(jnp.bfloat16)
        dk_ref[near, :] += lax.dot_general(
            score_grad, query, down, preferred_element_type=jnp.float32
        )
    dk = dk_ref[...]
    out_ref[:, lanes(base + HD)] = (dk * cosine - partner(dk) * sine).astype(jnp.bfloat16)
    out_ref[:, lanes(base + 2 * HD)] = dv_ref[...].astype(jnp.bfloat16)


def greet(axis, others):
    barrier = pltpu.get_barrier_semaphore()
    for other in others:
        pl.semaphore_signal(
            barrier, inc=1, device_id={axis: other}, device_id_type=pl.DeviceIdType.MESH
        )
    pl.semaphore_wait(barrier, len(others))


def attention_kernel(
    size, inputs_ref, saved_ref, gout_ref, cos_ref, sin_ref, bias_ref, out_ref, rows_ref,
    qkv_ref, grad_ref, dk_ref, dv_ref, send_sems, recv_sems, own_sems, send_rows, recv_rows,
):
    me = lax.axis_index("seq")
    tokens, columns = saved_ref.shape
    heads = columns // size // (3 * HD)
    others = [lax.rem(me + step, size) for step in range(1, size)]
    greet("seq", others)
    mine = pl.ds(pl.multiple_of(me * tokens, TILE), tokens)
    parts = ((saved_ref, qkv_ref, 3 * HD), (gout_ref, grad_ref, HD))

    def remote(source, target, send, recv, other):
        return pltpu.make_async_remote_copy(
            src_ref=source, dst_ref=target, send_sem=send, recv_sem=recv,
            device_id={"seq": other}, device_id_type=pl.DeviceIdType.MESH,
        )

    def piece(head, step, at):
        source, target, width = parts[at]
        other = others[step]
        there = pl.ds(pl.multiple_of((other * heads + head) * width, HD), width)
        here = pl.ds(pl.multiple_of(head * width, HD), width)
        return remote(
            source.at[:, there], target.at[mine, here],
            send_sems.at[head, step, at], recv_sems.at[head, step, at], other,
        )

    def own(head, at):
        source, target, width = parts[at]
        there = pl.ds(pl.multiple_of((me * heads + head) * width, HD), width)
        here = pl.ds(pl.multiple_of(head * width, HD), width)
        return pltpu.make_async_copy(
            source.at[:, there], target.at[mine, here], own_sems.at[head, at]
        )

    own_rows = pltpu.make_async_copy(inputs_ref, rows_ref.at[mine], own_sems.at[heads, 0])
    all_rows = [
        remote(inputs_ref, rows_ref.at[mine], send_rows.at[step], recv_rows.at[step], others[step])
        for step in range(size - 1)
    ]

    def launch(head, carry):
        for at in range(2):
            own(head, at).start()
        for step in range(size - 1):
            for at in range(2):
                piece(head, step, at).start()
        return carry

    lax.fori_loop(0, heads, launch, 0)
    for copy in all_rows:
        copy.start()
    own_rows.start()

    def work(head, carry):
        for at in range(2):
            own(head, at).wait()
        for step in range(size - 1):
            for at in range(2):
                piece(head, step, at).wait()
        head_backward(
            qkv_ref, grad_ref, cos_ref, sin_ref, bias_ref, out_ref, dk_ref, dv_ref, head
        )
        return carry

    lax.fori_loop(0, heads, work, 0)
    own_rows.wait()
    for copy in all_rows:
        copy.wait()


def attention(size, inputs, saved, gout, cosine, sine, bias):
    tokens = inputs.shape[0] * size
    heads = gout.shape[1] // size // HD
    vmem, anywhere = pl.BlockSpec(memory_space=pltpu.VMEM), pl.BlockSpec(memory_space=pl.ANY)
    dma = pltpu.SemaphoreType.DMA
    return pl.pallas_call(
        functools.partial(attention_kernel, size),
        out_shape=(
            jax.ShapeDtypeStruct((tokens, heads * 3 * HD), jnp.bfloat16),
            jax.ShapeDtypeStruct((tokens, inputs.shape[1]), jnp.bfloat16),
        ),
        in_specs=[anywhere] * 3 + [vmem] * 3,
        out_specs=(vmem, anywhere),
        scratch_shapes=[
            pltpu.VMEM((tokens, heads * 3 * HD), jnp.bfloat16),
            pltpu.VMEM((tokens, heads * HD), jnp.bfloat16),
            pltpu.VMEM((tokens, HD), jnp.float32),
            pltpu.VMEM((tokens, HD), jnp.float32),
            dma((heads, size - 1, 2)),
            dma((heads, size - 1, 2)),
            dma((heads + 1, 2)),
            dma((size - 1,)),
            dma((size - 1,)),
        ],
        compiler_params=pltpu.CompilerParams(
            collective_id=0, has_side_effects=True, vmem_limit_bytes=48 * 1024 * 1024
        ),
        cost_estimate=pl.CostEstimate(
            flops=heads * 10 * tokens * min(tokens, 768) * HD,
            bytes_accessed=100 * 1024 * 1024,
            transcendentals=heads * tokens * min(tokens, 768),
        ),
    )(inputs, saved, gout, cosine, sine, bias)


CUTS = 4


def grads_kernel(
    size, spread, grad_ref, weight_hbm, product_ref, out_ref, wout_ref,
    weight_ref, sent, landed, mine, paired, from_left, from_right,
    send_sems, recv_sems, weight_sem, own_sems, pair_send, pair_recv,
    left_send, left_recv, right_send, right_recv,
):
    me, row = lax.axis_index("seq"), lax.axis_index("fsdp")
    depth = spread // 2
    z, core = row // 2, row % 2
    chunks, width = sent.shape[0], sent.shape[2]
    tokens = out_ref.shape[0]
    height = wout_ref.shape[0]
    cut = height // CUTS
    others = [lax.rem(me + step, size) for step in range(1, size)]
    pair = row + 1 - 2 * core
    up, down = lax.rem(row + 2, spread), lax.rem(row + spread - 2, spread)

    barrier = pltpu.get_barrier_semaphore()

    def hail(axis, other):
        pl.semaphore_signal(
            barrier, inc=1, device_id={axis: other}, device_id_type=pl.DeviceIdType.MESH
        )

    for other in others:
        hail("seq", other)
    hail("fsdp", pair)
    hail("fsdp", down)
    hail("fsdp", up)
    pl.semaphore_wait(barrier, size + 2)

    load = pltpu.make_async_copy(weight_hbm, weight_ref, weight_sem)

    def rows_of(block, side, at):
        return pl.ds(pl.multiple_of((block * 2 + side) * height + at * cut, 16), cut)

    def part(at):
        return pl.ds(pl.multiple_of(at * cut, 16), cut)

    def own(block, at):
        return pltpu.make_async_copy(
            product_ref.at[rows_of(block, core, at)], mine.at[block, part(at)],
            own_sems.at[block, at],
        )

    def remote(source, target, send, recv, axis, other):
        return pltpu.make_async_remote_copy(
            src_ref=source, dst_ref=target, send_sem=send, recv_sem=recv,
            device_id={axis: other}, device_id_type=pl.DeviceIdType.MESH,
        )

    def to_pair(block, at):
        return remote(
            product_ref.at[rows_of(block, 1 - core, at)], paired.at[block, part(at)],
            pair_send.at[block, at], pair_recv.at[block, at], "fsdp", pair,
        )

    def to_up(block, at):
        return remote(
            mine.at[block, part(at)], from_left.at[block, part(at)],
            left_send.at[block, at], left_recv.at[block, at], "fsdp", up,
        )

    def to_down(block, at):
        return remote(
            mine.at[block, part(at)], from_right.at[block, part(at)],
            right_send.at[block, at], right_recv.at[block, at], "fsdp", down,
        )

    def piece(chunk, step):
        there = pl.ds(pl.multiple_of(others[step] * tokens, TILE), tokens)
        return remote(
            sent.at[chunk, there], landed.at[chunk, step],
            send_sems.at[chunk, step], recv_sems.at[chunk, step], "seq", others[step],
        )

    def launch(index, carry):
        turn, at = index // CUTS, index % CUTS
        half = turn // 2
        block = half + (1 - turn % 2) * (depth - 1 - 2 * half)
        to_pair(block, at).start()
        own(block, at).start()
        return carry

    lax.fori_loop(0, depth * CUTS, launch, 0)
    load.start()

    def pair_sum(block, at):
        own(block, at).wait()
        to_pair(block, at).wait()
        return mine[block, part(at), :].astype(jnp.float32) + paired[
            block, part(at), :
        ].astype(jnp.float32)

    def forward(block, at, has_behind, copy, behind):
        total = pair_sum(block, at)

        @pl.when(has_behind)
        def _():
            copy(block, at).wait_recv()
            more = total + behind[block, part(at), :].astype(jnp.float32)
            mine[block, part(at), :] = more.astype(jnp.bfloat16)

        @pl.when(jnp.logical_not(has_behind))
        def _():
            mine[block, part(at), :] = total.astype(jnp.bfloat16)

        copy(block, at).start()

    def product(chunk):
        here = pl.ds(pl.multiple_of(chunk * width, HD), width)
        sent[chunk] = lax.dot_general(
            grad_ref[...], weight_ref[here, :], (((1,), (1,)), ((), ())),
            preferred_element_type=jnp.float32,
        ).astype(jnp.bfloat16)
        for step in range(size - 1):
            piece(chunk, step).start()

    steps = (depth - 1) * CUTS

    def advance(index, carry):
        turn, at = index // CUTS, index % CUTS

        @pl.when(z < depth - 1 - turn)
        def _():
            forward(depth - 1 - turn, at, z > 0, to_up, from_left)

        @pl.when(z > turn)
        def _():
            forward(turn, at, z < depth - 1, to_down, from_right)

        @pl.when(index == 0)
        def _():
            load.wait()

        @pl.when(index < chunks)
        def _():
            product(index)

        return carry

    lax.fori_loop(0, steps, advance, 0)
    for chunk in range(steps, chunks):
        product(chunk)

    def add(chunk, carry):
        here = pl.ds(pl.multiple_of(chunk * width, HD), width)
        own_rows = pl.ds(pl.multiple_of(me * tokens, TILE), tokens)
        total = sent[chunk, own_rows].astype(jnp.float32)
        for step in range(size - 1):
            piece(chunk, step).wait()
            total = total + landed[chunk, step].astype(jnp.float32)
        out_ref[:, here] = total.astype(jnp.bfloat16)
        return carry

    lax.fori_loop(0, chunks, add, 0)

    def finish(at, carry):
        wout_ref[part(at), :] = pair_sum(z, at)

        @pl.when(z > 0)
        def _():
            to_up(z, at).wait_recv()
            wout_ref[part(at), :] += from_left[z, part(at), :].astype(jnp.float32)

        @pl.when(z < depth - 1)
        def _():
            to_down(z, at).wait_recv()
            wout_ref[part(at), :] += from_right[z, part(at), :].astype(jnp.float32)

        return carry

    lax.fori_loop(0, CUTS, finish, 0)

    def settle(index, carry):
        turn, at = index // CUTS, index % CUTS

        @pl.when(z < depth - 1 - turn)
        def _():
            to_up(depth - 1 - turn, at).wait_send()

        @pl.when(z > turn)
        def _():
            to_down(turn, at).wait_send()

        return carry

    lax.fori_loop(0, steps, settle, 0)


def both_grads(size, spread, qkv_grad, weight, product):
    tokens, columns = qkv_grad.shape
    model = weight.shape[0]
    width = 3 * HD
    chunks = model // width
    depth, height = spread // 2, model // spread
    vmem, anywhere = pl.BlockSpec(memory_space=pltpu.VMEM), pl.BlockSpec(memory_space=pl.ANY)
    dma = pltpu.SemaphoreType.DMA
    blocks = pltpu.VMEM((depth, height, columns), jnp.bfloat16)
    return pl.pallas_call(
        functools.partial(grads_kernel, size, spread),
        out_shape=(
            jax.ShapeDtypeStruct((tokens // size, model), jnp.bfloat16),
            jax.ShapeDtypeStruct((height, columns), jnp.float32),
        ),
        in_specs=[vmem, anywhere, anywhere],
        out_specs=(vmem, vmem),
        scratch_shapes=[
            pltpu.VMEM((model, columns), jnp.bfloat16),
            pltpu.VMEM((chunks, tokens, width), jnp.bfloat16),
            pltpu.VMEM((chunks, size - 1, tokens // size, width), jnp.bfloat16),
            blocks, blocks, blocks, blocks,
            dma((chunks, size - 1)),
            dma((chunks, size - 1)),
            dma,
        ]
        + [dma((depth, CUTS))] * 7,
        compiler_params=pltpu.CompilerParams(
            collective_id=1, has_side_effects=True, vmem_limit_bytes=58 * 1024 * 1024
        ),
        cost_estimate=pl.CostEstimate(
            flops=2 * tokens * columns * model,
            bytes_accessed=200 * 1024 * 1024,
            transcendentals=0,
        ),
    )(qkv_grad, weight, product)


def body(seq_size, fsdp_size, inputs, w_qkv, saved_qkv, out_grad, clip_grid, tile_pairs):
    window = tile_pairs[0]
    tile_count = window.shape[0]
    weight_full = lax.all_gather(w_qkv, "fsdp", axis=0, tiled=True)
    cosine, sine = rope_tables(clip_grid[0], tile_count)
    listed = jnp.any(
        window[:, :, None] == jnp.arange(tile_count, dtype=jnp.int32)[None, None, :], axis=1
    )
    bias = jnp.repeat(jnp.where(listed, 0.0, -1e30).astype(jnp.float32), TILE, axis=1)
    qkv_grad, group_rows = attention(
        seq_size, inputs[0], saved_qkv[0], out_grad[0], cosine, sine, bias
    )
    product = lax.dot_general(
        group_rows, qkv_grad, (((0,), (0,)), ((), ())), preferred_element_type=jnp.float32
    ).astype(jnp.bfloat16)
    input_grad, weight_grad = both_grads(seq_size, fsdp_size, qkv_grad, weight_full, product)
    return (input_grad[None], weight_grad)


def solution(mesh):
    in_specs = (
        P("fsdp", "seq", None),
        P("fsdp", "seq"),
        P("fsdp", "seq", None),
        P("fsdp", "seq", None),
        P("fsdp", None, None),
        P("fsdp", None, None),
    )
    out_specs = (P("fsdp", "seq", None), P("fsdp", "seq"))
    local = functools.partial(body, mesh.shape["seq"], mesh.shape["fsdp"])
    return jax.shard_map(local, mesh=mesh, in_specs=in_specs, out_specs=out_specs, check_vma=False)
```

```python
import functools

import jax
import jax.numpy as jnp
from jax import lax
from jax.experimental import pallas as pl
from jax.experimental.pallas import tpu as pltpu
from jax.sharding import PartitionSpec as P

HD = 128
RT = 16
RH = 56
RW = 56
TT = 2
TH = 8
TW = 8
AREA = 2
TILE = 128


ROPE_BASE = 256.0


def tile_places(layout, tile_count):
    tile_sizes = layout[:, 0] * layout[:, 1] * layout[:, 2]
    clip_ends = jnp.cumsum(tile_sizes, dtype=jnp.int32)
    clip_starts = clip_ends - tile_sizes
    tile_ids = jnp.arange(tile_count, dtype=jnp.int32)
    member = (
        (tile_ids[:, None] >= clip_starts[None, :]) & (tile_ids[:, None] < clip_ends[None, :])
    ).astype(jnp.int32)
    start_of = jnp.sum(member * clip_starts[None, :], axis=1, dtype=jnp.int32)
    rows_of = jnp.sum(member * layout[None, :, 1], axis=1, dtype=jnp.int32)
    cols_of = jnp.sum(member * layout[None, :, 2], axis=1, dtype=jnp.int32)
    local_id = tile_ids - start_of
    within = local_id % (rows_of * cols_of)
    return (local_id // (rows_of * cols_of), within // cols_of, within % cols_of)


def rope_tables(layout, tile_count):
    frame_tile, row_tile, column_tile = tile_places(layout, tile_count)
    inside = jnp.arange(TILE, dtype=jnp.int32)
    frame_pos = (frame_tile[:, None] * TT + (inside // (TH * TW))[None, :]).reshape(-1)
    row_pos = (row_tile[:, None] * TH + (inside // TW % TH)[None, :]).reshape(-1)
    column_pos = (column_tile[:, None] * TW + (inside % TW)[None, :]).reshape(-1)
    angles = []
    for position, section in ((frame_pos, RT), (row_pos, RH), (column_pos, RW)):
        ladder = jnp.arange(section // 2, dtype=jnp.float32) * (2.0 / section)
        frequency = jnp.exp(-jnp.log(jnp.float32(ROPE_BASE)) * ladder)
        spin_angle = position.astype(jnp.float32)[:, None] * frequency[None, :]
        angles += [spin_angle, spin_angle]
    all_angles = jnp.concatenate(angles, axis=1)
    signs = []
    for section in (RT, RH, RW):
        signs += [-jnp.ones((section // 2,), jnp.float32), jnp.ones((section // 2,), jnp.float32)]
    return (jnp.cos(all_angles), jnp.sin(all_angles) * jnp.concatenate(signs)[None, :])


def partner(values):
    lane = lax.broadcasted_iota(jnp.int32, values.shape, 1)
    short, long = RT // 2, RH // 2
    first = (lane < RT + long) | ((lane >= RT + RH) & (lane < RT + RH + long))
    wide = jnp.where(
        first, pltpu.roll(values, HD - long, 1), pltpu.roll(values, long, 1)
    )
    narrow = jnp.where(
        lane < short, pltpu.roll(values, HD - short, 1), pltpu.roll(values, short, 1)
    )
    return jnp.where(lane < RT, narrow, wide)


def head_backward(qkv_ref, grad_ref, cos_ref, sin_ref, bias_ref, out_ref, dk_ref, dv_ref, head):
    rows = AREA * TILE
    slabs = qkv_ref.shape[0] // rows
    scale = HD ** (-0.5)
    cosine, sine = cos_ref[...], sin_ref[...]

    def lanes(start, count=HD):
        return pl.ds(pl.multiple_of(start, HD), count)

    def rotated(start):
        values = qkv_ref[:, lanes(start)].astype(jnp.float32)
        return (values * cosine + partner(values) * sine).astype(jnp.bfloat16)

    base = head * (3 * HD)
    rot_q, rot_k = rotated(base), rotated(base + HD)
    values = qkv_ref[:, lanes(base + 2 * HD)]
    grads = grad_ref[:, lanes(head * HD)]
    across = (((1,), (1,)), ((), ()))
    plain = (((1,), (0,)), ((), ()))
    down = (((0,), (0,)), ((), ()))
    dk_ref[...] = jnp.zeros_like(dk_ref)
    dv_ref[...] = jnp.zeros_like(dv_ref)
    for slab in range(slabs):
        here = slice(slab * rows, (slab + 1) * rows)
        near = slice(max(0, slab - 1) * rows, min(slabs, slab + 2) * rows)
        width = near.stop - near.start
        query, grad, key, value = rot_q[here], grads[here], rot_k[near], values[near]
        bias = jnp.concatenate(
            [
                jnp.broadcast_to(bias_ref[tile : tile + 1, near], (TILE, width))
                for tile in range(slab * AREA, (slab + 1) * AREA)
            ],
            axis=0,
        )
        scores = lax.dot_general(query, key, across, preferred_element_type=jnp.float32)
        scores = scores * scale + bias
        expo = jnp.exp(scores - jnp.max(scores, axis=-1, keepdims=True))
        probs = expo * (1.0 / jnp.sum(expo, axis=-1, keepdims=True))
        dv_ref[near, :] += lax.dot_general(
            probs.astype(jnp.bfloat16), grad, down, preferred_element_type=jnp.float32
        )
        prob_grad = lax.dot_general(grad, value, across, preferred_element_type=jnp.float32)
        total = jnp.sum(probs * prob_grad, axis=-1, keepdims=True)
        score_grad = (probs * (prob_grad - total) * scale).astype(jnp.bfloat16)
        dq = lax.dot_general(score_grad, key, plain, preferred_element_type=jnp.float32)
        dq = dq * cosine[here] - partner(dq) * sine[here]
        out_ref[here, lanes(base)] = dq.astype(jnp.bfloat16)
        dk_ref[near, :] += lax.dot_general(
            score_grad, query, down, preferred_element_type=jnp.float32
        )
    dk = dk_ref[...]
    out_ref[:, lanes(base + HD)] = (dk * cosine - partner(dk) * sine).astype(jnp.bfloat16)
    out_ref[:, lanes(base + 2 * HD)] = dv_ref[...].astype(jnp.bfloat16)


def greet(axis, others):
    barrier = pltpu.get_barrier_semaphore()
    for other in others:
        pl.semaphore_signal(
            barrier, inc=1, device_id={axis: other}, device_id_type=pl.DeviceIdType.MESH
        )
    pl.semaphore_wait(barrier, len(others))


def attention_kernel(
    size, inputs_ref, saved_ref, gout_ref, cos_ref, sin_ref, bias_ref, out_ref, rows_ref,
    qkv_ref, grad_ref, dk_ref, dv_ref, send_sems, recv_sems, own_sems, send_rows, recv_rows,
):
    me = lax.axis_index("seq")
    tokens, columns = saved_ref.shape
    heads = columns // size // (3 * HD)
    others = [lax.rem(me + step, size) for step in range(1, size)]
    greet("seq", others)
    mine = pl.ds(pl.multiple_of(me * tokens, TILE), tokens)
    parts = ((saved_ref, qkv_ref, 3 * HD), (gout_ref, grad_ref, HD))

    def remote(source, target, send, recv, other):
        return pltpu.make_async_remote_copy(
            src_ref=source, dst_ref=target, send_sem=send, recv_sem=recv,
            device_id={"seq": other}, device_id_type=pl.DeviceIdType.MESH,
        )

    def piece(head, step, at):
        source, target, width = parts[at]
        other = others[step]
        there = pl.ds(pl.multiple_of((other * heads + head) * width, HD), width)
        here = pl.ds(pl.multiple_of(head * width, HD), width)
        return remote(
            source.at[:, there], target.at[mine, here],
            send_sems.at[head, step, at], recv_sems.at[head, step, at], other,
        )

    def own(head, at):
        source, target, width = parts[at]
        there = pl.ds(pl.multiple_of((me * heads + head) * width, HD), width)
        here = pl.ds(pl.multiple_of(head * width, HD), width)
        return pltpu.make_async_copy(
            source.at[:, there], target.at[mine, here], own_sems.at[head, at]
        )

    own_rows = pltpu.make_async_copy(inputs_ref, rows_ref.at[mine], own_sems.at[heads, 0])
    all_rows = [
        remote(inputs_ref, rows_ref.at[mine], send_rows.at[step], recv_rows.at[step], others[step])
        for step in range(size - 1)
    ]

    def launch(head, carry):
        for at in range(2):
            own(head, at).start()
        for step in range(size - 1):
            for at in range(2):
                piece(head, step, at).start()
        return carry

    lax.fori_loop(0, heads, launch, 0)
    for copy in all_rows:
        copy.start()
    own_rows.start()

    def work(head, carry):
        for at in range(2):
            own(head, at).wait()
        for step in range(size - 1):
            for at in range(2):
                piece(head, step, at).wait()
        head_backward(
            qkv_ref, grad_ref, cos_ref, sin_ref, bias_ref, out_ref, dk_ref, dv_ref, head
        )
        return carry

    lax.fori_loop(0, heads, work, 0)
    own_rows.wait()
    for copy in all_rows:
        copy.wait()


def attention(size, inputs, saved, gout, cosine, sine, bias):
    tokens = inputs.shape[0] * size
    heads = gout.shape[1] // size // HD
    vmem, anywhere = pl.BlockSpec(memory_space=pltpu.VMEM), pl.BlockSpec(memory_space=pl.ANY)
    dma = pltpu.SemaphoreType.DMA
    return pl.pallas_call(
        functools.partial(attention_kernel, size),
        out_shape=(
            jax.ShapeDtypeStruct((tokens, heads * 3 * HD), jnp.bfloat16),
            jax.ShapeDtypeStruct((tokens, inputs.shape[1]), jnp.bfloat16),
        ),
        in_specs=[anywhere] * 3 + [vmem] * 3,
        out_specs=(vmem, anywhere),
        scratch_shapes=[
            pltpu.VMEM((tokens, heads * 3 * HD), jnp.bfloat16),
            pltpu.VMEM((tokens, heads * HD), jnp.bfloat16),
            pltpu.VMEM((tokens, HD), jnp.float32),
            pltpu.VMEM((tokens, HD), jnp.float32),
            dma((heads, size - 1, 2)),
            dma((heads, size - 1, 2)),
            dma((heads + 1, 2)),
            dma((size - 1,)),
            dma((size - 1,)),
        ],
        compiler_params=pltpu.CompilerParams(
            collective_id=0, has_side_effects=True, vmem_limit_bytes=48 * 1024 * 1024
        ),
        cost_estimate=pl.CostEstimate(
            flops=heads * 10 * tokens * min(tokens, 768) * HD,
            bytes_accessed=100 * 1024 * 1024,
            transcendentals=heads * tokens * min(tokens, 768),
        ),
    )(inputs, saved, gout, cosine, sine, bias)


CUTS = 6


def pair_kernel(product_ref, out_ref, landed, own_sems, send_sems, recv_sems):
    row = lax.axis_index("fsdp")
    core = row % 2
    pair = row + 1 - 2 * core
    depth, height = out_ref.shape[0], out_ref.shape[1]
    barrier = pltpu.get_barrier_semaphore()
    pl.semaphore_signal(
        barrier, inc=1, device_id={"fsdp": pair}, device_id_type=pl.DeviceIdType.MESH
    )
    pl.semaphore_wait(barrier, 1)

    def rows_of(block, side):
        return pl.ds(pl.multiple_of((block * 2 + side) * height, 16), height)

    def own(block):
        return pltpu.make_async_copy(
            product_ref.at[rows_of(block, core)], out_ref.at[block], own_sems.at[block]
        )

    def across(block):
        return pltpu.make_async_remote_copy(
            src_ref=product_ref.at[rows_of(block, 1 - core)], dst_ref=landed.at[block],
            send_sem=send_sems.at[block], recv_sem=recv_sems.at[block],
            device_id={"fsdp": pair}, device_id_type=pl.DeviceIdType.MESH,
        )

    def launch(block, carry):
        across(block).start()
        own(block).start()
        return carry

    def add(block, carry):
        own(block).wait()
        across(block).wait()
        total = out_ref[block].astype(jnp.float32) + landed[block].astype(jnp.float32)
        out_ref[block] = total.astype(jnp.bfloat16)
        return carry

    lax.fori_loop(0, depth, launch, 0)
    lax.fori_loop(0, depth, add, 0)


def pair_sums(spread, product):
    model, columns = product.shape
    depth, height = spread // 2, model // spread
    dma = pltpu.SemaphoreType.DMA
    return pl.pallas_call(
        pair_kernel,
        out_shape=jax.ShapeDtypeStruct((depth, height, columns), jnp.bfloat16),
        in_specs=[pl.BlockSpec(memory_space=pl.ANY)],
        out_specs=pl.BlockSpec(memory_space=pltpu.VMEM),
        scratch_shapes=[pltpu.VMEM((depth, height, columns), jnp.bfloat16)]
        + [dma((depth,))] * 3,
        compiler_params=pltpu.CompilerParams(
            collective_id=2, has_side_effects=True, vmem_limit_bytes=32 * 1024 * 1024
        ),
        cost_estimate=pl.CostEstimate(
            flops=model * columns, bytes_accessed=8 * model * columns, transcendentals=0
        ),
    )(product)


def grads_kernel(
    size, spread, grad_ref, weight_hbm, product_ref, out_ref, wout_ref,
    weight_ref, sent, landed, mine, from_left, from_right,
    send_sems, recv_sems, weight_sem, own_sems,
    left_send, left_recv, right_send, right_recv,
):
    me, row = lax.axis_index("seq"), lax.axis_index("fsdp")
    depth = spread // 2
    z = row // 2
    chunks, width = sent.shape[0], sent.shape[2]
    tokens = out_ref.shape[0]
    height = wout_ref.shape[0]
    cut = height // CUTS
    others = [lax.rem(me + step, size) for step in range(1, size)]
    up, down = lax.rem(row + 2, spread), lax.rem(row + spread - 2, spread)

    barrier = pltpu.get_barrier_semaphore()

    def hail(axis, other):
        pl.semaphore_signal(
            barrier, inc=1, device_id={axis: other}, device_id_type=pl.DeviceIdType.MESH
        )

    for other in others:
        hail("seq", other)
    hail("fsdp", down)
    hail("fsdp", up)
    pl.semaphore_wait(barrier, size + 1)

    load = pltpu.make_async_copy(weight_hbm, weight_ref, weight_sem)

    def part(at):
        return pl.ds(pl.multiple_of(at * cut, 16), cut)

    def own(block, at):
        return pltpu.make_async_copy(
            product_ref.at[block, part(at)], mine.at[block, part(at)],
            own_sems.at[block, at],
        )

    def remote(source, target, send, recv, axis, other):
        return pltpu.make_async_remote_copy(
            src_ref=source, dst_ref=target, send_sem=send, recv_sem=recv,
            device_id={axis: other}, device_id_type=pl.DeviceIdType.MESH,
        )

    def to_up(block, at):
        return remote(
            mine.at[block, part(at)], from_left.at[block, part(at)],
            left_send.at[block, at], left_recv.at[block, at], "fsdp", up,
        )

    def to_down(block, at):
        return remote(
            mine.at[block, part(at)], from_right.at[block, part(at)],
            right_send.at[block, at], right_recv.at[block, at], "fsdp", down,
        )

    def piece(chunk, step):
        there = pl.ds(pl.multiple_of(others[step] * tokens, TILE), tokens)
        return remote(
            sent.at[chunk, there], landed.at[chunk, step],
            send_sems.at[chunk, step], recv_sems.at[chunk, step], "seq", others[step],
        )

    def launch(index, carry):
        turn, at = index // CUTS, index % CUTS
        half = turn // 2
        block = half + (1 - turn % 2) * (depth - 1 - 2 * half)
        own(block, at).start()
        return carry

    lax.fori_loop(0, depth * CUTS, launch, 0)
    load.start()

    def own_part(block, at):
        own(block, at).wait()
        return mine[block, part(at), :].astype(jnp.float32)

    def forward(block, at, has_behind, copy, behind):
        total = own_part(block, at)

        @pl.when(has_behind)
        def _():
            copy(block, at).wait_recv()
            more = total + behind[block, part(at), :].astype(jnp.float32)
            mine[block, part(at), :] = more.astype(jnp.bfloat16)

        @pl.when(jnp.logical_not(has_behind))
        def _():
            mine[block, part(at), :] = total.astype(jnp.bfloat16)

        copy(block, at).start()

    def product(chunk):
        here = pl.ds(pl.multiple_of(chunk * width, HD), width)
        sent[chunk] = lax.dot_general(
            grad_ref[...], weight_ref[here, :], (((1,), (1,)), ((), ())),
            preferred_element_type=jnp.float32,
        ).astype(jnp.bfloat16)
        for step in range(size - 1):
            piece(chunk, step).start()

    steps = (depth - 1) * CUTS

    def advance(index, carry):
        turn, at = index // CUTS, index % CUTS

        @pl.when(z < depth - 1 - turn)
        def _():
            forward(depth - 1 - turn, at, z > 0, to_up, from_left)

        @pl.when(z > turn)
        def _():
            forward(turn, at, z < depth - 1, to_down, from_right)

        @pl.when(index == 0)
        def _():
            load.wait()

        @pl.when(index < chunks)
        def _():
            product(index)

        return carry

    lax.fori_loop(0, steps, advance, 0)
    for chunk in range(steps, chunks):
        product(chunk)

    def add(chunk, carry):
        here = pl.ds(pl.multiple_of(chunk * width, HD), width)
        own_rows = pl.ds(pl.multiple_of(me * tokens, TILE), tokens)
        total = sent[chunk, own_rows].astype(jnp.float32)
        for step in range(size - 1):
            piece(chunk, step).wait()
            total = total + landed[chunk, step].astype(jnp.float32)
        out_ref[:, here] = total.astype(jnp.bfloat16)
        return carry

    lax.fori_loop(0, chunks, add, 0)

    def finish(at, carry):
        wout_ref[part(at), :] = own_part(z, at)

        @pl.when(z > 0)
        def _():
            to_up(z, at).wait_recv()
            wout_ref[part(at), :] += from_left[z, part(at), :].astype(jnp.float32)

        @pl.when(z < depth - 1)
        def _():
            to_down(z, at).wait_recv()
            wout_ref[part(at), :] += from_right[z, part(at), :].astype(jnp.float32)

        return carry

    lax.fori_loop(0, CUTS, finish, 0)

    def settle(index, carry):
        turn, at = index // CUTS, index % CUTS

        @pl.when(z < depth - 1 - turn)
        def _():
            to_up(depth - 1 - turn, at).wait_send()

        @pl.when(z > turn)
        def _():
            to_down(turn, at).wait_send()

        return carry

    lax.fori_loop(0, steps, settle, 0)


def both_grads(size, spread, qkv_grad, weight, product):
    tokens, columns = qkv_grad.shape
    model = weight.shape[0]
    width = 3 * HD
    chunks = model // width
    depth, height = spread // 2, model // spread
    vmem, anywhere = pl.BlockSpec(memory_space=pltpu.VMEM), pl.BlockSpec(memory_space=pl.ANY)
    dma = pltpu.SemaphoreType.DMA
    blocks = pltpu.VMEM((depth, height, columns), jnp.bfloat16)
    return pl.pallas_call(
        functools.partial(grads_kernel, size, spread),
        out_shape=(
            jax.ShapeDtypeStruct((tokens // size, model), jnp.bfloat16),
            jax.ShapeDtypeStruct((height, columns), jnp.float32),
        ),
        in_specs=[vmem, anywhere, anywhere],
        out_specs=(vmem, vmem),
        scratch_shapes=[
            pltpu.VMEM((model, columns), jnp.bfloat16),
            pltpu.VMEM((chunks, tokens, width), jnp.bfloat16),
            pltpu.VMEM((chunks, size - 1, tokens // size, width), jnp.bfloat16),
            blocks, blocks, blocks,
            dma((chunks, size - 1)),
            dma((chunks, size - 1)),
            dma,
        ]
        + [dma((depth, CUTS))] * 5,
        compiler_params=pltpu.CompilerParams(
            collective_id=1, has_side_effects=True, vmem_limit_bytes=58 * 1024 * 1024
        ),
        cost_estimate=pl.CostEstimate(
            flops=2 * tokens * columns * model,
            bytes_accessed=200 * 1024 * 1024,
            transcendentals=0,
        ),
    )(qkv_grad, weight, product)


def body(seq_size, fsdp_size, inputs, w_qkv, saved_qkv, out_grad, clip_grid, tile_pairs):
    window = tile_pairs[0]
    tile_count = window.shape[0]
    weight_full = lax.all_gather(w_qkv, "fsdp", axis=0, tiled=True)
    cosine, sine = rope_tables(clip_grid[0], tile_count)
    listed = jnp.any(
        window[:, :, None] == jnp.arange(tile_count, dtype=jnp.int32)[None, None, :], axis=1
    )
    bias = jnp.repeat(jnp.where(listed, 0.0, -1e30).astype(jnp.float32), TILE, axis=1)
    qkv_grad, group_rows = attention(
        seq_size, inputs[0], saved_qkv[0], out_grad[0], cosine, sine, bias
    )
    product = lax.dot_general(
        group_rows, qkv_grad, (((0,), (0,)), ((), ())), preferred_element_type=jnp.float32
    ).astype(jnp.bfloat16)
    summed = pair_sums(fsdp_size, product)
    input_grad, weight_grad = both_grads(seq_size, fsdp_size, qkv_grad, weight_full, summed)
    return (input_grad[None], weight_grad)


def solution(mesh):
    in_specs = (
        P("fsdp", "seq", None),
        P("fsdp", "seq"),
        P("fsdp", "seq", None),
        P("fsdp", "seq", None),
        P("fsdp", None, None),
        P("fsdp", None, None),
    )
    out_specs = (P("fsdp", "seq", None), P("fsdp", "seq"))
    local = functools.partial(body, mesh.shape["seq"], mesh.shape["fsdp"])
    return jax.shard_map(local, mesh=mesh, in_specs=in_specs, out_specs=out_specs, check_vma=False)
```

```python
import functools

import jax
import jax.numpy as jnp
from jax import lax
from jax.experimental import pallas as pl
from jax.experimental.pallas import tpu as pltpu
from jax.sharding import PartitionSpec as P

HD = 128
RT = 16
RH = 56
RW = 56
TT = 2
TH = 8
TW = 8
AREA = 2
TILE = 128


ROPE_BASE = 256.0


def tile_places(layout, tile_count):
    tile_sizes = layout[:, 0] * layout[:, 1] * layout[:, 2]
    clip_ends = jnp.cumsum(tile_sizes, dtype=jnp.int32)
    clip_starts = clip_ends - tile_sizes
    tile_ids = jnp.arange(tile_count, dtype=jnp.int32)
    member = (
        (tile_ids[:, None] >= clip_starts[None, :]) & (tile_ids[:, None] < clip_ends[None, :])
    ).astype(jnp.int32)
    start_of = jnp.sum(member * clip_starts[None, :], axis=1, dtype=jnp.int32)
    rows_of = jnp.sum(member * layout[None, :, 1], axis=1, dtype=jnp.int32)
    cols_of = jnp.sum(member * layout[None, :, 2], axis=1, dtype=jnp.int32)
    local_id = tile_ids - start_of
    within = local_id % (rows_of * cols_of)
    return (local_id // (rows_of * cols_of), within // cols_of, within % cols_of)


def rope_tables(layout, tile_count):
    frame_tile, row_tile, column_tile = tile_places(layout, tile_count)
    inside = jnp.arange(TILE, dtype=jnp.int32)
    frame_pos = (frame_tile[:, None] * TT + (inside // (TH * TW))[None, :]).reshape(-1)
    row_pos = (row_tile[:, None] * TH + (inside // TW % TH)[None, :]).reshape(-1)
    column_pos = (column_tile[:, None] * TW + (inside % TW)[None, :]).reshape(-1)
    angles = []
    for position, section in ((frame_pos, RT), (row_pos, RH), (column_pos, RW)):
        ladder = jnp.arange(section // 2, dtype=jnp.float32) * (2.0 / section)
        frequency = jnp.exp(-jnp.log(jnp.float32(ROPE_BASE)) * ladder)
        spin_angle = position.astype(jnp.float32)[:, None] * frequency[None, :]
        angles += [spin_angle, spin_angle]
    all_angles = jnp.concatenate(angles, axis=1)
    signs = []
    for section in (RT, RH, RW):
        signs += [-jnp.ones((section // 2,), jnp.float32), jnp.ones((section // 2,), jnp.float32)]
    return (jnp.cos(all_angles), jnp.sin(all_angles) * jnp.concatenate(signs)[None, :])


def partner(values):
    lane = lax.broadcasted_iota(jnp.int32, values.shape, 1)
    short, long = RT // 2, RH // 2
    first = (lane < RT + long) | ((lane >= RT + RH) & (lane < RT + RH + long))
    wide = jnp.where(
        first, pltpu.roll(values, HD - long, 1), pltpu.roll(values, long, 1)
    )
    narrow = jnp.where(
        lane < short, pltpu.roll(values, HD - short, 1), pltpu.roll(values, short, 1)
    )
    return jnp.where(lane < RT, narrow, wide)


def head_backward(qkv_ref, grad_ref, cos_ref, sin_ref, bias_ref, out_ref, dk_ref, dv_ref, head):
    rows = AREA * TILE
    slabs = qkv_ref.shape[0] // rows
    scale = HD ** (-0.5)
    cosine, sine = cos_ref[...], sin_ref[...]

    def lanes(start, count=HD):
        return pl.ds(pl.multiple_of(start, HD), count)

    def rotated(start):
        values = qkv_ref[:, lanes(start)].astype(jnp.float32)
        return (values * cosine + partner(values) * sine).astype(jnp.bfloat16)

    base = head * (3 * HD)
    rot_q, rot_k = rotated(base), rotated(base + HD)
    values = qkv_ref[:, lanes(base + 2 * HD)]
    grads = grad_ref[:, lanes(head * HD)]
    across = (((1,), (1,)), ((), ()))
    plain = (((1,), (0,)), ((), ()))
    down = (((0,), (0,)), ((), ()))
    dk_ref[...] = jnp.zeros_like(dk_ref)
    dv_ref[...] = jnp.zeros_like(dv_ref)
    for slab in range(slabs):
        here = slice(slab * rows, (slab + 1) * rows)
        near = slice(max(0, slab - 1) * rows, min(slabs, slab + 2) * rows)
        width = near.stop - near.start
        query, grad, key, value = rot_q[here], grads[here], rot_k[near], values[near]
        bias = jnp.concatenate(
            [
                jnp.broadcast_to(bias_ref[tile : tile + 1, near], (TILE, width))
                for tile in range(slab * AREA, (slab + 1) * AREA)
            ],
            axis=0,
        )
        scores = lax.dot_general(query, key, across, preferred_element_type=jnp.float32)
        scores = scores * scale + bias
        expo = jnp.exp(scores - jnp.max(scores, axis=-1, keepdims=True))
        probs = expo * (1.0 / jnp.sum(expo, axis=-1, keepdims=True))
        dv_ref[near, :] += lax.dot_general(
            probs.astype(jnp.bfloat16), grad, down, preferred_element_type=jnp.float32
        )
        prob_grad = lax.dot_general(grad, value, across, preferred_element_type=jnp.float32)
        total = jnp.sum(probs * prob_grad, axis=-1, keepdims=True)
        score_grad = (probs * (prob_grad - total) * scale).astype(jnp.bfloat16)
        dq = lax.dot_general(score_grad, key, plain, preferred_element_type=jnp.float32)
        dq = dq * cosine[here] - partner(dq) * sine[here]
        out_ref[here, lanes(base)] = dq.astype(jnp.bfloat16)
        dk_ref[near, :] += lax.dot_general(
            score_grad, query, down, preferred_element_type=jnp.float32
        )
    dk = dk_ref[...]
    out_ref[:, lanes(base + HD)] = (dk * cosine - partner(dk) * sine).astype(jnp.bfloat16)
    out_ref[:, lanes(base + 2 * HD)] = dv_ref[...].astype(jnp.bfloat16)


def greet(axis, others):
    barrier = pltpu.get_barrier_semaphore()
    for other in others:
        pl.semaphore_signal(
            barrier, inc=1, device_id={axis: other}, device_id_type=pl.DeviceIdType.MESH
        )
    pl.semaphore_wait(barrier, len(others))


def attention_kernel(
    size, inputs_ref, saved_ref, gout_ref, cos_ref, sin_ref, bias_ref, out_ref, rows_ref,
    qkv_ref, grad_ref, dk_ref, dv_ref, send_sems, recv_sems, own_sems, send_rows, recv_rows,
):
    me = lax.axis_index("seq")
    tokens, columns = saved_ref.shape
    heads = columns // size // (3 * HD)
    others = [lax.rem(me + step, size) for step in range(1, size)]
    greet("seq", others)
    mine = pl.ds(pl.multiple_of(me * tokens, TILE), tokens)
    parts = ((saved_ref, qkv_ref, 3 * HD), (gout_ref, grad_ref, HD))

    def remote(source, target, send, recv, other):
        return pltpu.make_async_remote_copy(
            src_ref=source, dst_ref=target, send_sem=send, recv_sem=recv,
            device_id={"seq": other}, device_id_type=pl.DeviceIdType.MESH,
        )

    def piece(head, step, at):
        source, target, width = parts[at]
        other = others[step]
        there = pl.ds(pl.multiple_of((other * heads + head) * width, HD), width)
        here = pl.ds(pl.multiple_of(head * width, HD), width)
        return remote(
            source.at[:, there], target.at[mine, here],
            send_sems.at[head, step, at], recv_sems.at[head, step, at], other,
        )

    def own(head, at):
        source, target, width = parts[at]
        there = pl.ds(pl.multiple_of((me * heads + head) * width, HD), width)
        here = pl.ds(pl.multiple_of(head * width, HD), width)
        return pltpu.make_async_copy(
            source.at[:, there], target.at[mine, here], own_sems.at[head, at]
        )

    own_rows = pltpu.make_async_copy(inputs_ref, rows_ref.at[mine], own_sems.at[heads, 0])
    all_rows = [
        remote(inputs_ref, rows_ref.at[mine], send_rows.at[step], recv_rows.at[step], others[step])
        for step in range(size - 1)
    ]

    def launch(head, carry):
        for at in range(2):
            own(head, at).start()
        for step in range(size - 1):
            for at in range(2):
                piece(head, step, at).start()
        return carry

    lax.fori_loop(0, heads, launch, 0)
    for copy in all_rows:
        copy.start()
    own_rows.start()

    def work(head, carry):
        for at in range(2):
            own(head, at).wait()
        for step in range(size - 1):
            for at in range(2):
                piece(head, step, at).wait()
        head_backward(
            qkv_ref, grad_ref, cos_ref, sin_ref, bias_ref, out_ref, dk_ref, dv_ref, head
        )
        return carry

    lax.fori_loop(0, heads, work, 0)
    own_rows.wait()
    for copy in all_rows:
        copy.wait()


def attention(size, inputs, saved, gout, cosine, sine, bias):
    tokens = inputs.shape[0] * size
    heads = gout.shape[1] // size // HD
    vmem, anywhere = pl.BlockSpec(memory_space=pltpu.VMEM), pl.BlockSpec(memory_space=pl.ANY)
    dma = pltpu.SemaphoreType.DMA
    return pl.pallas_call(
        functools.partial(attention_kernel, size),
        out_shape=(
            jax.ShapeDtypeStruct((tokens, heads * 3 * HD), jnp.bfloat16),
            jax.ShapeDtypeStruct((tokens, inputs.shape[1]), jnp.bfloat16),
        ),
        in_specs=[anywhere] * 3 + [vmem] * 3,
        out_specs=(vmem, anywhere),
        scratch_shapes=[
            pltpu.VMEM((tokens, heads * 3 * HD), jnp.bfloat16),
            pltpu.VMEM((tokens, heads * HD), jnp.bfloat16),
            pltpu.VMEM((tokens, HD), jnp.float32),
            pltpu.VMEM((tokens, HD), jnp.float32),
            dma((heads, size - 1, 2)),
            dma((heads, size - 1, 2)),
            dma((heads + 1, 2)),
            dma((size - 1,)),
            dma((size - 1,)),
        ],
        compiler_params=pltpu.CompilerParams(
            collective_id=0, has_side_effects=True, vmem_limit_bytes=48 * 1024 * 1024
        ),
        cost_estimate=pl.CostEstimate(
            flops=heads * 10 * tokens * min(tokens, 768) * HD,
            bytes_accessed=100 * 1024 * 1024,
            transcendentals=heads * tokens * min(tokens, 768),
        ),
    )(inputs, saved, gout, cosine, sine, bias)


CUTS = 3


def grads_kernel(
    size, spread, grad_ref, weight_hbm, product_ref, out_ref, wout_ref,
    weight_ref, sent, landed, mine, paired, from_left, from_right,
    send_sems, recv_sems, weight_sem, own_sems, pair_send, pair_recv,
    left_send, left_recv, right_send, right_recv,
):
    me, row = lax.axis_index("seq"), lax.axis_index("fsdp")
    depth = spread // 2
    z, core = row // 2, row % 2
    chunks, width = sent.shape[0], sent.shape[2]
    tokens = out_ref.shape[0]
    height = wout_ref.shape[0]
    cut = height // CUTS
    others = [lax.rem(me + step, size) for step in range(1, size)]
    pair = row + 1 - 2 * core
    up, down = lax.rem(row + 2, spread), lax.rem(row + spread - 2, spread)

    barrier = pltpu.get_barrier_semaphore()

    def hail(axis, other):
        pl.semaphore_signal(
            barrier, inc=1, device_id={axis: other}, device_id_type=pl.DeviceIdType.MESH
        )

    for other in others:
        hail("seq", other)
    hail("fsdp", pair)
    hail("fsdp", down)
    hail("fsdp", up)
    pl.semaphore_wait(barrier, size + 2)

    load = pltpu.make_async_copy(weight_hbm, weight_ref, weight_sem)

    def rows_of(block, side, at):
        return pl.ds(pl.multiple_of((block * 2 + side) * height + at * cut, 16), cut)

    def part(at):
        return pl.ds(pl.multiple_of(at * cut, 16), cut)

    def own(block, at):
        return pltpu.make_async_copy(
            product_ref.at[rows_of(block, core, at)], mine.at[block, part(at)],
            own_sems.at[block, at],
        )

    def remote(source, target, send, recv, axis, other):
        return pltpu.make_async_remote_copy(
            src_ref=source, dst_ref=target, send_sem=send, recv_sem=recv,
            device_id={axis: other}, device_id_type=pl.DeviceIdType.MESH,
        )

    def to_pair(block, at):
        return remote(
            product_ref.at[rows_of(block, 1 - core, at)], paired.at[block, part(at)],
            pair_send.at[block, at], pair_recv.at[block, at], "fsdp", pair,
        )

    def to_up(block, at):
        return remote(
            mine.at[block, part(at)], from_left.at[block, part(at)],
            left_send.at[block, at], left_recv.at[block, at], "fsdp", up,
        )

    def to_down(block, at):
        return remote(
            mine.at[block, part(at)], from_right.at[block, part(at)],
            right_send.at[block, at], right_recv.at[block, at], "fsdp", down,
        )

    def piece(chunk, step):
        there = pl.ds(pl.multiple_of(others[step] * tokens, TILE), tokens)
        return remote(
            sent.at[chunk, there], landed.at[chunk, step],
            send_sems.at[chunk, step], recv_sems.at[chunk, step], "seq", others[step],
        )

    def launch(index, carry):
        turn, at = index // CUTS, index % CUTS
        half = turn // 2
        block = half + (1 - turn % 2) * (depth - 1 - 2 * half)
        to_pair(block, at).start()
        own(block, at).start()
        return carry

    lax.fori_loop(0, depth * CUTS, launch, 0)
    load.start()

    def pair_sum(block, at):
        own(block, at).wait()
        to_pair(block, at).wait()
        return mine[block, part(at), :].astype(jnp.float32) + paired[
            block, part(at), :
        ].astype(jnp.float32)

    def forward(block, at, has_behind, copy, behind):
        total = pair_sum(block, at)

        @pl.when(has_behind)
        def _():
            copy(block, at).wait_recv()
            more = total + behind[block, part(at), :].astype(jnp.float32)
            mine[block, part(at), :] = more.astype(jnp.bfloat16)

        @pl.when(jnp.logical_not(has_behind))
        def _():
            mine[block, part(at), :] = total.astype(jnp.bfloat16)

        copy(block, at).start()

    def product(chunk):
        here = pl.ds(pl.multiple_of(chunk * width, HD), width)
        sent[chunk] = lax.dot_general(
            grad_ref[...], weight_ref[here, :], (((1,), (1,)), ((), ())),
            preferred_element_type=jnp.float32,
        ).astype(jnp.bfloat16)
        for step in range(size - 1):
            piece(chunk, step).start()

    steps = (depth - 1) * CUTS

    def advance(index, carry):
        turn, at = index // CUTS, index % CUTS

        @pl.when(z < depth - 1 - turn)
        def _():
            forward(depth - 1 - turn, at, z > 0, to_up, from_left)

        @pl.when(z > turn)
        def _():
            forward(turn, at, z < depth - 1, to_down, from_right)

        @pl.when(index == 0)
        def _():
            load.wait()

        @pl.when(index < chunks)
        def _():
            product(index)

        return carry

    lax.fori_loop(0, steps, advance, 0)
    for chunk in range(steps, chunks):
        product(chunk)

    def add(chunk, carry):
        here = pl.ds(pl.multiple_of(chunk * width, HD), width)
        own_rows = pl.ds(pl.multiple_of(me * tokens, TILE), tokens)
        total = sent[chunk, own_rows].astype(jnp.float32)
        for step in range(size - 1):
            piece(chunk, step).wait()
            total = total + landed[chunk, step].astype(jnp.float32)
        out_ref[:, here] = total.astype(jnp.bfloat16)
        return carry

    lax.fori_loop(0, chunks, add, 0)

    def finish(at, carry):
        wout_ref[part(at), :] = pair_sum(z, at)

        @pl.when(z > 0)
        def _():
            to_up(z, at).wait_recv()
            wout_ref[part(at), :] += from_left[z, part(at), :].astype(jnp.float32)

        @pl.when(z < depth - 1)
        def _():
            to_down(z, at).wait_recv()
            wout_ref[part(at), :] += from_right[z, part(at), :].astype(jnp.float32)

        return carry

    lax.fori_loop(0, CUTS, finish, 0)

    def settle(index, carry):
        turn, at = index // CUTS, index % CUTS

        @pl.when(z < depth - 1 - turn)
        def _():
            to_up(depth - 1 - turn, at).wait_send()

        @pl.when(z > turn)
        def _():
            to_down(turn, at).wait_send()

        return carry

    lax.fori_loop(0, steps, settle, 0)


def both_grads(size, spread, qkv_grad, weight, product):
    tokens, columns = qkv_grad.shape
    model = weight.shape[0]
    width = 3 * HD
    chunks = model // width
    depth, height = spread // 2, model // spread
    vmem, anywhere = pl.BlockSpec(memory_space=pltpu.VMEM), pl.BlockSpec(memory_space=pl.ANY)
    dma = pltpu.SemaphoreType.DMA
    blocks = pltpu.VMEM((depth, height, columns), jnp.bfloat16)
    return pl.pallas_call(
        functools.partial(grads_kernel, size, spread),
        out_shape=(
            jax.ShapeDtypeStruct((tokens // size, model), jnp.bfloat16),
            jax.ShapeDtypeStruct((height, columns), jnp.float32),
        ),
        in_specs=[vmem, anywhere, anywhere],
        out_specs=(vmem, vmem),
        scratch_shapes=[
            pltpu.VMEM((model, columns), jnp.bfloat16),
            pltpu.VMEM((chunks, tokens, width), jnp.bfloat16),
            pltpu.VMEM((chunks, size - 1, tokens // size, width), jnp.bfloat16),
            blocks, blocks, blocks, blocks,
            dma((chunks, size - 1)),
            dma((chunks, size - 1)),
            dma,
        ]
        + [dma((depth, CUTS))] * 7,
        compiler_params=pltpu.CompilerParams(
            collective_id=1, has_side_effects=True, vmem_limit_bytes=58 * 1024 * 1024
        ),
        cost_estimate=pl.CostEstimate(
            flops=2 * tokens * columns * model,
            bytes_accessed=200 * 1024 * 1024,
            transcendentals=0,
        ),
    )(qkv_grad, weight, product)


def body(seq_size, fsdp_size, inputs, w_qkv, saved_qkv, out_grad, clip_grid, tile_pairs):
    window = tile_pairs[0]
    tile_count = window.shape[0]
    weight_full = lax.all_gather(w_qkv, "fsdp", axis=0, tiled=True)
    cosine, sine = rope_tables(clip_grid[0], tile_count)
    listed = jnp.any(
        window[:, :, None] == jnp.arange(tile_count, dtype=jnp.int32)[None, None, :], axis=1
    )
    bias = jnp.repeat(jnp.where(listed, 0.0, -1e30).astype(jnp.float32), TILE, axis=1)
    qkv_grad, group_rows = attention(
        seq_size, inputs[0], saved_qkv[0], out_grad[0], cosine, sine, bias
    )
    product = lax.dot_general(
        group_rows, qkv_grad, (((0,), (0,)), ((), ())), preferred_element_type=jnp.float32
    ).astype(jnp.bfloat16)
    input_grad, weight_grad = both_grads(seq_size, fsdp_size, qkv_grad, weight_full, product)
    return (input_grad[None], weight_grad)


def solution(mesh):
    in_specs = (
        P("fsdp", "seq", None),
        P("fsdp", "seq"),
        P("fsdp", "seq", None),
        P("fsdp", "seq", None),
        P("fsdp", None, None),
        P("fsdp", None, None),
    )
    out_specs = (P("fsdp", "seq", None), P("fsdp", "seq"))
    local = functools.partial(body, mesh.shape["seq"], mesh.shape["fsdp"])
    return jax.shard_map(local, mesh=mesh, in_specs=in_specs, out_specs=out_specs, check_vma=False)
```
